32 devices in a mesh: loop: 4 (over y, x), grp: 8 (over z, core).
Axes of the slice: x: 2, y: 2, z: 4, core: 2. Of those that a mesh axis runs over, the one named last changes fastest.
Arguments:
- queries: bfloat16 [4096, 4096], P(('loop', 'grp')), as said below
- passages: bfloat16 [2048, 4096], P(('loop', 'grp')), as said below
- pool: bfloat16 [8192, 4096], P(('loop', 'grp')), as said below
- query_count: int32 [4, 8], P('loop', 'grp'), may hold values from 32 to 128, as said below
- positive: int32 [4096], P(('loop', 'grp')), may hold values from 0 to 255
- neg_owner: int32 [4096, 7], P(('loop', 'grp')), may hold values from 0 to 7, as said below
- neg_row: int32 [4096, 7], P(('loop', 'grp')), may hold values from 0 to 255
Outputs:
- loss: float32 [4096], P(('loop', 'grp'))
- grad_query: float32 [4096, 4096], P(('loop', 'grp'))
- grad_passage: float32 [2048, 4096], P(('loop', 'grp'))
- grad_pool: float32 [8192, 4096], P(('loop', 'grp'))
The draws below stay inside these ranges and needn't reach their ends.
Inputs may be any that keep to these rules, and one draw needn't show every extreme that they name: `queries`: every entry lies in -0.25 to 0.25. `passages`: every entry lies in -0.25 to 0.25. `pool`: every entry lies in -0.25 to 0.25. `query_count`: some device has all 128 slots live. `neg_owner`: among the 896 entries of one device, at most 140 name one owner; for every loop index one owner is named exactly 140 times by every device of that loop index. Entries of slots that are not live are present too.
All inputs are finite; a program needn't handle non-finite values.
Results may differ from the reference program's by a relative error of at most 0.02.
Values may be sent and summed in bfloat16 or wider, within the bound.
A program may use at most 192 MiB of HBM per device.

```python
import jax
import jax.numpy as jnp
from jax import lax

D = 4096
Q_DEV = 128
P_DEV = 64
HN = 7
CAP = 140
POOL_DEV = 256
QUERIES = 4096
PASSAGES = 2048
POOL = 8192
N_LOOP = 4
N_GRP = 8


positive_share = 0.13


negative_share = 0.08


noise_share = 0.3


def topic_total():
    return min(32, POOL_DEV)


def topic_table(key):
    return jax.random.normal(jax.random.fold_in(key, 77), (topic_total(), D), jnp.float32)


def passage_topics(key):
    return jax.random.randint(jax.random.fold_in(key, 11), (PASSAGES,), 0, topic_total()).astype(jnp.int32)


def pool_layout(key):
    block_total = N_LOOP * N_GRP
    block_keys = jax.random.split(jax.random.fold_in(key, 12), block_total)

    def one_layout(single_key):
        return jax.random.permutation(single_key, POOL_DEV).astype(jnp.int32)
    return jax.vmap(one_layout)(block_keys)


def pool_topics(key):
    layout = pool_layout(key)
    labels = (jnp.arange(POOL_DEV, dtype=jnp.int32) % topic_total()).astype(jnp.int32)

    def one_block(placed):
        return jnp.zeros((POOL_DEV,), jnp.int32).at[placed].set(labels)
    return jax.vmap(one_block)(layout).reshape(POOL)


def positive_table(key):
    return jax.random.randint(jax.random.fold_in(key, 13), (QUERIES,), 0, N_LOOP * P_DEV).astype(jnp.int32)


def query_blocks():
    block_index = jnp.arange(QUERIES, dtype=jnp.int32) // Q_DEV
    return (block_index // N_GRP, block_index % N_GRP)


def query_topics(key):
    chosen = positive_table(key)
    loop_index, group_index = query_blocks()
    source = (chosen // P_DEV * N_GRP + group_index) * P_DEV + chosen % P_DEV
    return (passage_topics(key)[source], source)


def owner_table(key):
    slot_total = Q_DEV * HN
    tickets = N_GRP * CAP
    busiest = jax.random.randint(jax.random.fold_in(key, 9), (N_LOOP,), 0, N_GRP)

    def one_device(device):
        first, second = jax.random.split(jax.random.fold_in(key, 100 + device))
        labels = (jnp.arange(tickets) // CAP + busiest[device // N_GRP]) % N_GRP
        others = CAP + jax.random.permutation(first, tickets - CAP)
        picked = jnp.concatenate([jnp.arange(CAP), others[:slot_total - CAP]])
        shuffle = jax.random.permutation(second, slot_total)
        return labels[picked][shuffle].reshape(Q_DEV, HN)
    owners = jax.vmap(one_device)(jnp.arange(N_LOOP * N_GRP))
    return owners.reshape(QUERIES, HN).astype(jnp.int32)


def row_table(key):
    owners = owner_table(key)
    topics, unused = query_topics(key)
    layout = pool_layout(key)
    loop_index, group_index = query_blocks()
    owner_block = loop_index[:, None] * N_GRP + owners
    spread = jax.random.randint(jax.random.fold_in(key, 14), (QUERIES, HN), 0, POOL_DEV // topic_total())
    position = topics[:, None] + topic_total() * spread
    return layout[owner_block, position].astype(jnp.int32)


def noise_rows(key, salt, count):
    noise_key = jax.random.fold_in(key, salt)
    return jax.random.normal(noise_key, (count, D), jnp.float32)


def finish(mixed):
    return jnp.clip(mixed * 0.015625, -0.25, 0.25).astype(jnp.bfloat16)


def draw_passages(key, part):
    table = topic_table(key)
    mixed = table[passage_topics(key)] + noise_rows(key, 2, PASSAGES)
    return finish(mixed)


def draw_pool(key, part):
    table = topic_table(key)
    mixed = table[pool_topics(key)] + noise_rows(key, 3, POOL)
    return finish(mixed)


def draw_queries(key, part):
    table = topic_table(key)
    topics, source = query_topics(key)
    passage_noise = noise_rows(key, 2, PASSAGES)
    pool_noise = noise_rows(key, 3, POOL)
    owners = owner_table(key)
    pool_rows = row_table(key)
    loop_index, group_index = query_blocks()
    flat = (loop_index[:, None] * N_GRP + owners) * POOL_DEV + pool_rows
    mixed = table[topics]
    mixed = mixed + positive_share * passage_noise[source] + noise_share * noise_rows(key, 1, QUERIES)
    for column in range(HN):
        mixed = mixed + negative_share * pool_noise[flat[:, column]]
    return finish(mixed)


def draw_query_count(key, part):
    first, second = jax.random.split(jax.random.fold_in(key, 5))
    devices = N_LOOP * N_GRP
    counts = jax.random.randint(first, (devices,), max(1, Q_DEV // 4), Q_DEV + 1)
    full = jax.random.randint(second, (), 0, devices)
    counts = jnp.where(jnp.arange(devices) == full, Q_DEV, counts)
    return counts.reshape(N_LOOP, N_GRP).astype(jnp.int32)


def draw_positive(key, part):
    return positive_table(key)


def draw_neg_owner(key, part):
    return owner_table(key)


def draw_neg_row(key, part):
    return row_table(key)


def setup_inputs(seed: int = 0) -> dict:
    key_list = jax.random.split(jax.random.key(seed), 8)
    return {
        "queries": draw_queries(jax.random.fold_in(key_list[7], 71), 0),
        "passages": draw_passages(jax.random.fold_in(key_list[7], 71), 0),
        "pool": draw_pool(jax.random.fold_in(key_list[7], 71), 0),
        "query_count": draw_query_count(jax.random.fold_in(key_list[7], 71), 0),
        "positive": draw_positive(jax.random.fold_in(key_list[7], 71), 0),
        "neg_owner": draw_neg_owner(jax.random.fold_in(key_list[7], 71), 0),
        "neg_row": draw_neg_row(jax.random.fold_in(key_list[7], 71), 0),
    }


inv_temp = 50.0
eps = 1e-06

def unit_rows(rows):
    scale = lax.rsqrt(lax.optimization_barrier(jnp.sum(rows * rows, axis=-1, keepdims=True)) + eps)
    return (rows * scale, scale)

def unit_back(grad, unit, scale):
    return (grad - unit * lax.optimization_barrier(jnp.sum(unit * grad, axis=-1, keepdims=True))) * scale

def to_groups(x, inner):
    rest = x.shape[1:]
    shaped = x.reshape((N_LOOP, N_GRP, inner) + rest)
    order = (1, 0) + tuple(range(2, shaped.ndim))
    return shaped.transpose(order).reshape((N_GRP, N_LOOP * inner) + rest)

def from_groups(x, inner):
    rest = x.shape[2:]
    shaped = x.reshape((N_GRP, N_LOOP, inner) + rest)
    order = (1, 0) + tuple(range(2, shaped.ndim))
    return shaped.transpose(order).reshape((N_LOOP * N_GRP * inner,) + rest)

def reference(queries, passages, pool, query_count, positive, neg_owner, neg_row):
    q_unit, q_scale = unit_rows(queries.astype(jnp.float32))
    p_unit, p_scale = unit_rows(passages.astype(jnp.float32))
    n_unit, n_scale = unit_rows(pool.astype(jnp.float32))
    q_hat = q_unit.astype(jnp.bfloat16)
    p_hat = p_unit.astype(jnp.bfloat16)
    n_hat = n_unit.astype(jnp.bfloat16)
    live = jnp.arange(Q_DEV, dtype=jnp.int32)[None, None, :] < query_count[:, :, None]
    valid_groups = live.astype(jnp.float32).transpose(1, 0, 2).reshape(N_GRP, N_LOOP * Q_DEV)
    loop_of = jnp.arange(N_LOOP * Q_DEV, dtype=jnp.int32) // Q_DEV
    slots_in = N_LOOP * P_DEV
    columns = jnp.arange(slots_in, dtype=jnp.int32)

    def per_group(pool_sum, inputs):
        q_grp, p_grp, pos_grp, owner_grp, row_grp, valid_grp = inputs
        flat = ((loop_of[:, None] * N_GRP + owner_grp) * POOL_DEV + row_grp).astype(jnp.int32)
        negs = n_hat[flat]
        scores = jnp.dot(q_grp, p_grp.T, preferred_element_type=jnp.float32) * inv_temp
        hard = jnp.einsum('qd,qkd->qk', q_grp.astype(jnp.float32), negs.astype(jnp.float32)) * inv_temp
        weights_in = jnp.exp(scores - inv_temp)
        weights_hard = jnp.exp(hard - inv_temp)
        total = lax.optimization_barrier(jnp.sum(weights_in, axis=1)) + lax.optimization_barrier(jnp.sum(weights_hard, axis=1))
        chosen = jnp.take_along_axis(scores, pos_grp[:, None], axis=1)[:, 0]
        loss = valid_grp * (jnp.log(total) + inv_temp - chosen)
        target = (pos_grp[:, None] == columns[None, :]).astype(jnp.float32)
        valid_col = valid_grp[:, None]
        coef_in = (valid_col * (weights_in / total[:, None] - target)).astype(jnp.bfloat16)
        coef_hard = (valid_col * weights_hard / total[:, None]).astype(jnp.bfloat16)
        in_part = jnp.dot(coef_in, p_grp, preferred_element_type=jnp.float32)
        hard_part = jnp.einsum('qk,qkd->qd', coef_hard.astype(jnp.float32), negs.astype(jnp.float32))
        dq_hat = inv_temp * (in_part + hard_part)
        dp_hat = inv_temp * jnp.dot(coef_in.T, q_grp, preferred_element_type=jnp.float32)
        neg_grad = (inv_temp * coef_hard.astype(jnp.float32)[:, :, None] * q_grp.astype(jnp.float32)[:, None, :]).astype(jnp.bfloat16)
        pool_sum = pool_sum.at[flat.reshape(-1)].add(neg_grad.astype(jnp.float32).reshape(-1, D))
        return (pool_sum, (loss, dq_hat, dp_hat))
    inputs = (to_groups(q_hat, Q_DEV), to_groups(p_hat, P_DEV), to_groups(positive, Q_DEV), to_groups(neg_owner, Q_DEV), to_groups(neg_row, Q_DEV), valid_groups)
    start = jnp.zeros((POOL, D), jnp.float32)
    pool_sum, (loss, dq_hat, dp_hat) = lax.scan(per_group, start, inputs)
    loss = from_groups(loss, Q_DEV)
    grad_query = unit_back(from_groups(dq_hat, Q_DEV), q_unit, q_scale)
    grad_passage = unit_back(from_groups(dp_hat, P_DEV), p_unit, p_scale)
    grad_pool = unit_back(pool_sum, n_unit, n_scale)
    return (loss, grad_query, grad_passage, grad_pool)
```

```python
import jax
import jax.numpy as jnp
from jax import lax
from jax.sharding import PartitionSpec as P

inv_temp = 50.0
eps = 1e-06


def unit_rows(rows):
    scale = lax.rsqrt(jnp.sum(rows * rows, axis=-1, keepdims=True) + eps)
    return (rows * scale, scale)


def unit_back(grad, unit, scale):
    return (grad - unit * jnp.sum(unit * grad, axis=-1, keepdims=True)) * scale


def cross(left, right):
    return lax.dot_general(
        left, right, (((1,), (1,)), ((), ())), preferred_element_type=jnp.float32
    )


def gather_back(coef, rows):
    return lax.dot_general(coef, rows, (((0,), (0,)), ((), ())), preferred_element_type=jnp.float32)


def local(queries, passages, pool, query_count, positive, neg_owner, neg_row):
    n_query, width = queries.shape
    n_pass = passages.shape[0]
    n_pool = pool.shape[0]
    groups = lax.axis_size("grp")
    loops = lax.axis_size("loop")
    me = lax.axis_index("grp")
    q_unit, q_scale = unit_rows(queries.astype(jnp.float32))
    p_unit, p_scale = unit_rows(passages.astype(jnp.float32))
    n_unit, n_scale = unit_rows(pool.astype(jnp.float32))
    q_hat = q_unit.astype(jnp.bfloat16)
    p_hat = p_unit.astype(jnp.bfloat16)
    n_hat = n_unit.astype(jnp.bfloat16)
    valid = lax.iota(jnp.int32, n_query) < query_count.reshape(())
    codes = jnp.where(valid[:, None], neg_owner * n_pool + neg_row, -1)
    valid = valid.astype(jnp.float32)[:, None]
    q_all = lax.all_gather(q_hat, "grp", axis=0, tiled=True)
    p_all = lax.all_gather(p_hat, "loop", axis=0, tiled=True)
    codes_all = lax.all_gather(codes, "grp", axis=0, tiled=True)

    scores = cross(q_hat, p_all) * inv_temp
    weights_in = jnp.exp(scores - inv_temp)
    total_in = jnp.sum(weights_in, axis=1)
    chosen = jnp.take_along_axis(scores, positive[:, None], axis=1)[:, 0]

    mine = me * n_pool + lax.iota(jnp.int32, n_pool)
    count = jnp.sum((codes_all[:, :, None] == mine[None, None, :]).astype(jnp.float32), axis=1)
    weights_hard = jnp.exp(cross(q_all, n_hat) * inv_temp - inv_temp)
    part = jnp.sum(weights_hard * count, axis=1)
    part = part + jnp.where(
        lax.iota(jnp.int32, groups)[:, None] == me, total_in[None, :], 0.0
    ).reshape(-1)
    total_all = lax.psum(part, "grp")
    total = lax.dynamic_slice_in_dim(total_all, me * n_query, n_query, 0)
    loss = valid[:, 0] * (jnp.log(total) + inv_temp - chosen)
    target = (positive[:, None] == lax.iota(jnp.int32, loops * n_pass)[None, :]).astype(jnp.float32)
    coef_in = (valid * (weights_in / total[:, None] - target)).astype(jnp.bfloat16)
    coef_hard = (count * (weights_hard / total_all[:, None])).astype(jnp.bfloat16)

    hard_part = jnp.dot(coef_hard, n_hat, preferred_element_type=jnp.float32).astype(jnp.bfloat16)
    hard_part = lax.psum_scatter(hard_part, "grp", scatter_dimension=0, tiled=True)
    pass_part = gather_back(coef_in, q_hat).astype(jnp.bfloat16)
    pass_part = lax.psum_scatter(pass_part, "loop", scatter_dimension=0, tiled=True)
    in_part = jnp.dot(coef_in, p_all, preferred_element_type=jnp.float32)
    pool_sum = gather_back(coef_hard, q_all)
    grad_query = unit_back(inv_temp * (in_part + hard_part.astype(jnp.float32)), q_unit, q_scale)
    grad_passage = unit_back(inv_temp * pass_part.astype(jnp.float32), p_unit, p_scale)
    grad_pool = unit_back(inv_temp * pool_sum, n_unit, n_scale)
    return (loss, grad_query, grad_passage, grad_pool)


def solution(mesh):
    return jax.shard_map(
        local,
        mesh=mesh,
        in_specs=(
            P(("loop", "grp"), None),
            P(("loop", "grp"), None),
            P(("loop", "grp"), None),
            P("loop", "grp"),
            P(("loop", "grp")),
            P(("loop", "grp"), None),
            P(("loop", "grp"), None),
        ),
        out_specs=(
            P(("loop", "grp")),
            P(("loop", "grp"), None),
            P(("loop", "grp"), None),
            P(("loop", "grp"), None),
        ),
        check_vma=False,
    )
```

```python
import functools

import jax
import jax.numpy as jnp
from jax import lax
from jax.experimental import pallas as pl
from jax.experimental.pallas import tpu as pltpu
from jax.sharding import PartitionSpec as P

inv_temp = 50.0
eps = 1e-06
parts = 4
tile = 512


def unit_rows(rows):
    scale = lax.rsqrt(jnp.sum(rows * rows, axis=-1, keepdims=True) + eps)
    return (rows * scale, scale)


def unit_back(grad, unit, scale):
    return (grad - unit * jnp.sum(unit * grad, axis=-1, keepdims=True)) * scale


def cross(left, right):
    return lax.dot_general(
        left, right, (((1,), (1,)), ((), ())), preferred_element_type=jnp.float32
    )


def plain(left, right):
    return jnp.dot(left, right, preferred_element_type=jnp.float32)


def kernel(
    loops, chips,
    q_ref, p_ref, n_ref, code_ref, pos_ref, live_ref,
    loss_ref, dq_ref, dp_ref, dn_ref,
    q_all, n_sib, p_all, codes, weights, coef, totals,
    d_part, d_recv, dp_part, dp_recv, dn_part, dn_recv,
    ag_s, ag_r, rs_s, rs_r, tot_s, tot_r, code_s, code_r,
    p_s, p_r, dp_s, dp_r, sib_s, sib_r,
):
    loop = lax.axis_index("loop")
    me = lax.axis_index("grp")
    z = me // 2
    core = me % 2
    sib = z * 2 + 1 - core
    n_query, width = q_ref.shape
    n_pass = p_ref.shape[0]
    n_pool = n_ref.shape[0]
    rows = n_query // parts
    lanes = chips * rows
    passages = loops * n_pass
    tiles = width // tile

    def at_chip(chip):
        return (loop, chip * 2 + core)

    def peer_chip(off):
        return lax.rem(z + off, chips)

    def peer_loop(off):
        return lax.rem(loop + off, loops)

    def remote(src, dst, send, recv, device):
        return pltpu.make_async_remote_copy(
            src_ref=src, dst_ref=dst, send_sem=send, recv_sem=recv,
            device_id=device, device_id_type=pl.DeviceIdType.MESH,
        )

    barrier = pltpu.get_barrier_semaphore()
    for off in range(1, chips):
        pl.semaphore_signal(barrier, inc=1, device_id=at_chip(peer_chip(off)),
                            device_id_type=pl.DeviceIdType.MESH)
    for off in range(1, loops):
        pl.semaphore_signal(barrier, inc=1, device_id=(peer_loop(off), me),
                            device_id_type=pl.DeviceIdType.MESH)
    pl.semaphore_signal(barrier, inc=1, device_id=(loop, sib),
                        device_id_type=pl.DeviceIdType.MESH)
    pl.semaphore_wait(barrier, chips + loops - 1)

    def ag_copy(part, block, up, own=False):
        src = q_ref.at[pl.ds(part * rows, rows)] if own else q_all.at[part, block]
        way = 0 if up else 1
        chip = z + 1 if up else z - 1
        return remote(src, q_all.at[part, block], ag_s.at[part, block, way],
                      ag_r.at[part, block], at_chip(chip))

    def ag_own(part):
        @pl.when(z < chips - 1)
        def _():
            ag_copy(part, z, True, own=True).start()

        @pl.when(z > 0)
        def _():
            ag_copy(part, z, False, own=True).start()

    def ag_slot(part, step):
        @pl.when(z - step >= 0)
        def _():
            ag_copy(part, z - step, True).wait_recv()

            @pl.when(z < chips - 1)
            def _():
                ag_copy(part, z - step, True).start()

        @pl.when(z + step < chips)
        def _():
            ag_copy(part, z + step, False).wait_recv()

            @pl.when(z > 0)
            def _():
                ag_copy(part, z + step, False).start()

    def ag_drain(part):
        for step in range(chips):
            @pl.when((z - step >= 0) & (z < chips - 1))
            def _():
                ag_copy(part, z - step, True, own=step == 0).wait_send()

            @pl.when((z + step < chips) & (z > 0))
            def _():
                ag_copy(part, z + step, False, own=step == 0).wait_send()

    def rs_up(part, target):
        return remote(d_part.at[part, target], d_recv.at[part, target],
                      rs_s.at[part, target], rs_r.at[part, target], at_chip(z + 1))

    def rs_down(part, target):
        slot = jnp.where(target == z - 1, chips, target)
        return remote(d_part.at[part, target], d_recv.at[part, slot],
                      rs_s.at[part, target], rs_r.at[part, slot], at_chip(z - 1))

    def rs_arrived(part, slot):
        remote(d_part.at[part, 0], d_recv.at[part, slot],
               rs_s.at[part, 0], rs_r.at[part, slot], at_chip(z)).wait_recv()

    def rs_start(part):
        @pl.when(z == 0)
        def _():
            for target in range(chips - 1, 0, -1):
                rs_up(part, target).start()

        @pl.when(z == chips - 1)
        def _():
            for target in range(chips - 1):
                rs_down(part, target).start()

    def rs_add(part, target):
        d_part[part, target] = (
            d_part[part, target].astype(jnp.float32) + d_recv[part, target].astype(jnp.float32)
        ).astype(jnp.bfloat16)

    def rs_slot(part, step):
        @pl.when((z >= 1) & (step >= z))
        def _():
            target = chips - 1 - step + z
            rs_arrived(part, target)

            @pl.when(target > z)
            def _():
                rs_add(part, target)
                rs_up(part, target).start()

        @pl.when((z < chips - 1) & (step >= chips - 1 - z))
        def _():
            target = step - (chips - 1) + z
            rs_arrived(part, jnp.where(target == z, chips, target))

            @pl.when(target < z)
            def _():
                rs_add(part, target)
                rs_down(part, target).start()

    def rs_finish(part):
        mine = pl.ds(part * rows, rows)
        dq_ref[mine, :] = inv_temp * d_part[part, z].astype(jnp.float32)

        @pl.when(z > 0)
        def _():
            dq_ref[mine, :] += inv_temp * d_recv[part, z].astype(jnp.float32)

        @pl.when(z < chips - 1)
        def _():
            dq_ref[mine, :] += inv_temp * d_recv[part, chips].astype(jnp.float32)

    def rs_drain(part):
        for target in range(chips):
            @pl.when(z != target)
            def _():
                rs_up(part, target).wait_send()

    def tot_copy(part, off):
        return remote(totals.at[part, z], totals.at[part, z], tot_s.at[part, off],
                      tot_r.at[part, z], at_chip(peer_chip(off)))

    def code_copy(off):
        return remote(code_ref, codes.at[z], code_s.at[off], code_r.at[z],
                      at_chip(peer_chip(off)))

    def pass_copy(off):
        return remote(p_ref, p_all.at[loop], p_s.at[off], p_r.at[loop],
                      (peer_loop(off), me))

    def dp_copy(off):
        to = peer_loop(off)
        return remote(dp_part.at[to], dp_recv.at[loop], dp_s.at[off], dp_r.at[loop],
                      (to, me))

    pool_copy = remote(n_ref, n_sib, sib_s.at[0], sib_r.at[0], (loop, sib))
    dn_copy = remote(dn_part, dn_recv, sib_s.at[1], sib_r.at[1], (loop, sib))

    def q_cols(part, cols):
        return q_all[part, :, :, cols].reshape(lanes, tile)

    def p_cols(cols):
        return p_all[:, :, cols].reshape(passages, tile)

    def columns(i):
        return pl.ds(pl.multiple_of(i * tile, tile), tile)

    ag_own(0)
    for off in range(1, chips):
        code_copy(off).start()
    for off in range(1, loops):
        pass_copy(off).start()
    pool_copy.start()
    ag_own(1)
    for part in range(parts):
        q_all[part, z] = q_ref[pl.ds(part * rows, rows), :]
    p_all[loop] = p_ref[...]
    codes[z] = code_ref[...]
    for step in range(1, chips):
        ag_slot(0, step)
    for off in range(1, chips):
        chip = peer_chip(off)
        remote(code_ref, codes.at[chip], code_s.at[off], code_r.at[chip],
               at_chip(chip)).wait_recv()
    pool_copy.wait_recv()
    for off in range(1, loops):
        other = peer_loop(off)
        remote(p_ref, p_all.at[other], p_s.at[off], p_r.at[other], (other, me)).wait_recv()

    own_lane = lax.broadcasted_iota(jnp.int32, (1, lanes), 1) // rows == z
    top, bottom, end = n_pool, 2 * n_pool, 2 * n_pool + passages

    for part in range(parts):
        def add_scores(i, carry):
            cols = columns(i)
            q_tile = q_cols(part, cols)
            return (
                carry[0] + cross(n_ref[:, cols], q_tile),
                carry[1] + cross(n_sib[:, cols], q_tile),
                carry[2] + cross(p_cols(cols), q_tile),
            )

        s_own, s_sib, s_in = lax.fori_loop(
            0, tiles, add_scores,
            (jnp.zeros((n_pool, lanes), jnp.float32), jnp.zeros((n_pool, lanes), jnp.float32),
             jnp.zeros((passages, lanes), jnp.float32)),
        )
        part_codes = codes[0, part]
        for chip in range(1, chips):
            here = lax.broadcasted_iota(jnp.int32, part_codes.shape, 1) // rows == chip
            part_codes = jnp.where(here, codes[chip, part], part_codes)
        row_id = lax.broadcasted_iota(jnp.int32, (n_pool, lanes), 0)
        for first, owner, score in ((0, me, s_own), (top, sib, s_sib)):
            ids = row_id + owner * n_pool
            count = jnp.zeros((n_pool, lanes), jnp.float32)
            for k in range(part_codes.shape[0]):
                count += jnp.where(part_codes[k:k + 1, :] == ids, 1.0, 0.0)
            weights[0, first:first + n_pool, :] = count
            weights[1, first:first + n_pool, :] = jnp.exp(score * inv_temp - inv_temp)
        s_in = s_in * inv_temp
        weights[1, bottom:end, :] = jnp.exp(s_in - inv_temp)
        target = lax.broadcasted_iota(jnp.int32, (passages, lanes), 0) == pos_ref[part, 0:1, :]
        chosen = jnp.sum(jnp.where(target, s_in, 0.0), axis=0, keepdims=True)
        in_total = jnp.sum(weights[1, bottom:end, :], axis=0, keepdims=True)
        hard_total = jnp.sum(weights[0, 0:bottom, :] * weights[1, 0:bottom, :], axis=0,
                             keepdims=True)
        mine = hard_total + jnp.where(own_lane, in_total, 0.0)
        totals[part, z] = jnp.broadcast_to(mine, (8, lanes))
        for off in range(1, chips):
            tot_copy(part, off).start()

        if part + 2 < parts:
            ag_own(part + 2)
        for step in range(1, chips):
            if part + 1 < parts:
                ag_slot(part + 1, step)
            if part >= 1:
                rs_slot(part - 1, step)

        for off in range(1, chips):
            chip = peer_chip(off)
            remote(totals.at[part, z], totals.at[part, chip], tot_s.at[part, off],
                   tot_r.at[part, chip], at_chip(chip)).wait_recv()
        total = totals[part, 0, 0:1, :]
        for chip in range(1, chips):
            total = total + totals[part, chip, 0:1, :]
        live = live_ref[part, 0:1, :]
        loss_ref[part] = jnp.broadcast_to(
            jnp.where(own_lane, live * (jnp.log(total) + inv_temp - chosen), 0.0), (8, lanes)
        )
        share = weights[1, 0:bottom, :] / total
        share = share.astype(jnp.bfloat16).astype(jnp.float32) * weights[0, 0:bottom, :]
        inside = weights[1, bottom:end, :] / total - jnp.where(target, 1.0, 0.0)
        inside = jnp.where(own_lane, live * inside, 0.0)
        place = pl.ds(part * lanes, lanes)
        coef[0:bottom, place] = share.astype(jnp.bfloat16)
        coef[bottom:end, place] = inside.astype(jnp.bfloat16)
        back = jnp.transpose(share).astype(jnp.bfloat16)
        back_in = jnp.transpose(inside).astype(jnp.bfloat16)

        @pl.loop(0, tiles)
        def _(i):
            cols = columns(i)
            grad = plain(back[:, 0:top], n_ref[:, cols])
            grad += plain(back[:, top:bottom], n_sib[:, cols])
            grad += plain(back_in, p_cols(cols))
            d_part[part, :, :, cols] = grad.astype(jnp.bfloat16).reshape(chips, rows, tile)

        rs_start(part)

    def q_whole(cols):
        return q_all[:, :, :, cols].reshape(parts * lanes, tile)

    @pl.loop(0, tiles)
    def _(i):
        cols = columns(i)
        grad = plain(coef[bottom:end, :], q_whole(cols))
        dp_part[:, :, cols] = grad.astype(jnp.bfloat16).reshape(loops, n_pass, tile)

    for off in range(1, loops):
        dp_copy(off).start()
    rs_slot(parts - 1, 1)

    @pl.loop(0, tiles)
    def _(i):
        cols = columns(i)
        dn_part[:, cols] = plain(coef[top:bottom, :], q_whole(cols)).astype(jnp.bfloat16)

    dn_copy.start()
    for step in range(2, chips - 1):
        rs_slot(parts - 1, step)

    @pl.loop(0, tiles)
    def _(i):
        cols = columns(i)
        dn_ref[:, cols] = inv_temp * plain(coef[0:top, :], q_whole(cols))

    for part in range(parts - 1):
        rs_finish(part)
    dn_copy.wait_recv()

    @pl.loop(0, tiles)
    def _(i):
        cols = columns(i)
        dn_ref[:, cols] += inv_temp * dn_recv[:, cols].astype(jnp.float32)

    if chips > 2:
        rs_slot(parts - 1, chips - 1)
    dp_ref[...] = inv_temp * dp_part[loop].astype(jnp.float32)
    for off in range(1, loops):
        other = peer_loop(off)
        remote(dp_part.at[other], dp_recv.at[other], dp_s.at[off], dp_r.at[other],
               (other, me)).wait_recv()
        dp_ref[...] += inv_temp * dp_recv[other].astype(jnp.float32)
    rs_finish(parts - 1)

    for part in range(parts):
        ag_drain(part)
        rs_drain(part)
        for off in range(1, chips):
            tot_copy(part, off).wait_send()
    for off in range(1, chips):
        code_copy(off).wait_send()
    for off in range(1, loops):
        pass_copy(off).wait_send()
        dp_copy(off).wait_send()
    pool_copy.wait_send()
    dn_copy.wait_send()


def local(queries, passages, pool, query_count, positive, neg_owner, neg_row):
    n_query, width = queries.shape
    n_pass = passages.shape[0]
    n_pool = pool.shape[0]
    hard_count = neg_owner.shape[1]
    loops = lax.axis_size("loop")
    chips = lax.axis_size("grp") // 2
    rows = n_query // parts
    lanes = chips * rows
    q_unit, q_scale = unit_rows(queries.astype(jnp.float32))
    p_unit, p_scale = unit_rows(passages.astype(jnp.float32))
    n_unit, n_scale = unit_rows(pool.astype(jnp.float32))
    q_hat = q_unit.astype(jnp.bfloat16)
    p_hat = p_unit.astype(jnp.bfloat16)
    n_hat = n_unit.astype(jnp.bfloat16)
    valid = lax.iota(jnp.int32, n_query) < query_count.reshape(())

    def spread(flat):
        cut = jnp.transpose(flat.reshape(parts, rows, -1), (0, 2, 1))
        return jnp.tile(cut, (1, 1, chips))

    wanted = jnp.where(valid[:, None], neg_owner * n_pool + neg_row, -1)
    wanted = jnp.pad(wanted, ((0, 0), (0, -hard_count % 8)), constant_values=-1)
    wanted = spread(wanted)
    pos = jnp.broadcast_to(spread(positive[:, None]), (parts, 8, lanes))
    live = jnp.broadcast_to(spread(valid.astype(jnp.float32)[:, None]), (parts, 8, lanes))
    vmem = pl.BlockSpec(memory_space=pltpu.VMEM)
    dma = pltpu.SemaphoreType.DMA
    bf16, f32 = jnp.bfloat16, jnp.float32
    all_rows = 2 * n_pool + loops * n_pass
    loss, dq, dp, dn = pl.pallas_call(
        functools.partial(kernel, loops, chips),
        out_shape=(
            jax.ShapeDtypeStruct((parts, 8, lanes), f32),
            jax.ShapeDtypeStruct((n_query, width), f32),
            jax.ShapeDtypeStruct((n_pass, width), f32),
            jax.ShapeDtypeStruct((n_pool, width), f32),
        ),
        in_specs=[vmem] * 6,
        out_specs=(vmem,) * 4,
        scratch_shapes=[
            pltpu.VMEM((parts, chips, rows, width), bf16),
            pltpu.VMEM((n_pool, width), bf16),
            pltpu.VMEM((loops, n_pass, width), bf16),
            pltpu.VMEM((chips,) + wanted.shape, jnp.int32),
            pltpu.VMEM((2, all_rows, lanes), f32),
            pltpu.VMEM((all_rows, parts * lanes), bf16),
            pltpu.VMEM((parts, chips, 8, lanes), f32),
            pltpu.VMEM((parts, chips, rows, width), bf16),
            pltpu.VMEM((parts, chips + 1, rows, width), bf16),
            pltpu.VMEM((loops, n_pass, width), bf16),
            pltpu.VMEM((loops, n_pass, width), bf16),
            pltpu.VMEM((n_pool, width), bf16),
            pltpu.VMEM((n_pool, width), bf16),
            dma((parts, chips, 2)),
            dma((parts, chips)),
            dma((parts, chips)),
            dma((parts, chips + 1)),
            dma((parts, chips)),
            dma((parts, chips)),
            dma((chips,)),
            dma((chips,)),
            dma((loops,)),
            dma((loops,)),
            dma((loops,)),
            dma((loops,)),
            dma((2,)),
            dma((2,)),
        ],
        compiler_params=pltpu.CompilerParams(
            collective_id=0, has_side_effects=True, vmem_limit_bytes=62 * 1024 * 1024
        ),
    )(q_hat, p_hat, n_hat, wanted, pos, live)
    loss = jnp.sum(loss[:, 0, :].reshape(parts, chips, rows), axis=1).reshape(n_query)
    grad_query = unit_back(dq, q_unit, q_scale)
    grad_passage = unit_back(dp, p_unit, p_scale)
    grad_pool = unit_back(dn, n_unit, n_scale)
    return (loss, grad_query, grad_passage, grad_pool)


def solution(mesh):
    return jax.shard_map(
        local,
        mesh=mesh,
        in_specs=(
            P(("loop", "grp"), None),
            P(("loop", "grp"), None),
            P(("loop", "grp"), None),
            P("loop", "grp"),
            P(("loop", "grp")),
            P(("loop", "grp"), None),
            P(("loop", "grp"), None),
        ),
        out_specs=(
            P(("loop", "grp")),
            P(("loop", "grp"), None),
            P(("loop", "grp"), None),
            P(("loop", "grp"), None),
        ),
        check_vma=False,
    )
```

```python
import functools

import jax
import jax.numpy as jnp
from jax import lax
from jax.experimental import pallas as pl
from jax.experimental.pallas import tpu as pltpu
from jax.sharding import PartitionSpec as P

inv_temp = 50.0
eps = 1e-06
parts = 4
tile = 512
strip = 16


def scale_of(rows):
    return lax.rsqrt(jnp.sum(rows * rows, axis=-1, keepdims=True) + eps)


def unit_back(grad, raw):
    raw = raw.astype(jnp.float32)
    scale = scale_of(raw)
    unit = raw * scale
    return (grad - unit * jnp.sum(unit * grad, axis=-1, keepdims=True)) * scale


def cross(left, right):
    return lax.dot_general(
        left, right, (((1,), (1,)), ((), ())), preferred_element_type=jnp.float32
    )


def plain(left, right):
    return jnp.dot(left, right, preferred_element_type=jnp.float32)


def kernel(
    loops, chips,
    q_ref, p_ref, n_ref, code_ref, pos_ref, live_ref,
    loss_ref, dq_ref, dp_ref, dn_ref,
    q_all, n_own, n_sib, p_all, q_loop, codes, weights, coef, totals,
    d_part, d_recv, c_part, c_recv, dn_part, dn_recv,
    ag_s, ag_r, rs_s, rs_r, tot_s, tot_r, code_s, code_r,
    p_s, p_r, ql_s, ql_r, c_s, c_r, sib_s, sib_r,
):
    loop = lax.axis_index("loop")
    me = lax.axis_index("grp")
    z = me // 2
    core = me % 2
    sib = z * 2 + 1 - core
    n_query, width = q_ref.shape
    n_pass = p_ref.shape[0]
    n_pool = n_ref.shape[0]
    rows = n_query // parts
    lanes = chips * rows
    passages = loops * n_pass
    tiles = width // tile

    def at_chip(chip):
        return (loop, chip * 2 + core)

    def peer_chip(off):
        return lax.rem(z + off, chips)

    def peer_loop(off):
        return lax.rem(loop + off, loops)

    def remote(src, dst, send, recv, device):
        return pltpu.make_async_remote_copy(
            src_ref=src, dst_ref=dst, send_sem=send, recv_sem=recv,
            device_id=device, device_id_type=pl.DeviceIdType.MESH,
        )

    barrier = pltpu.get_barrier_semaphore()
    for off in range(1, chips):
        pl.semaphore_signal(barrier, inc=1, device_id=at_chip(peer_chip(off)),
                            device_id_type=pl.DeviceIdType.MESH)
    for off in range(1, loops):
        pl.semaphore_signal(barrier, inc=1, device_id=(peer_loop(off), me),
                            device_id_type=pl.DeviceIdType.MESH)
    pl.semaphore_signal(barrier, inc=1, device_id=(loop, sib),
                        device_id_type=pl.DeviceIdType.MESH)

    def unit_strip(raw):
        raw = raw.astype(jnp.float32)
        return (raw * scale_of(raw)).astype(jnp.bfloat16)

    def unit_queries(part):
        for low in range(0, rows, strip):
            q_all[part, z, low:low + strip, :] = unit_strip(
                q_ref[part * rows + low:part * rows + low + strip, :])

    unit_queries(0)
    pl.semaphore_wait(barrier, chips + loops - 1)

    def ag_copy(part, block, up):
        way = 0 if up else 1
        chip = z + 1 if up else z - 1
        return remote(q_all.at[part, block], q_all.at[part, block], ag_s.at[part, block, way],
                      ag_r.at[part, block], at_chip(chip))

    def ag_own(part):
        @pl.when(z < chips - 1)
        def _():
            ag_copy(part, z, True).start()

        @pl.when(z > 0)
        def _():
            ag_copy(part, z, False).start()

    def ag_slot(part, step):
        @pl.when(z - step >= 0)
        def _():
            ag_copy(part, z - step, True).wait_recv()

            @pl.when(z < chips - 1)
            def _():
                ag_copy(part, z - step, True).start()

        @pl.when(z + step < chips)
        def _():
            ag_copy(part, z + step, False).wait_recv()

            @pl.when(z > 0)
            def _():
                ag_copy(part, z + step, False).start()

    def ag_drain(part):
        for step in range(chips):
            @pl.when((z - step >= 0) & (z < chips - 1))
            def _():
                ag_copy(part, z - step, True).wait_send()

            @pl.when((z + step < chips) & (z > 0))
            def _():
                ag_copy(part, z + step, False).wait_send()

    def rs_up(part, target):
        return remote(d_part.at[part, target], d_recv.at[part, target],
                      rs_s.at[part, target], rs_r.at[part, target], at_chip(z + 1))

    def rs_down(part, target):
        slot = jnp.where(target == z - 1, chips, target)
        return remote(d_part.at[part, target], d_recv.at[part, slot],
                      rs_s.at[part, target], rs_r.at[part, slot], at_chip(z - 1))

    def rs_arrived(part, slot):
        remote(d_part.at[part, 0], d_recv.at[part, slot],
               rs_s.at[part, 0], rs_r.at[part, slot], at_chip(z)).wait_recv()

    def rs_start(part):
        @pl.when(z == 0)
        def _():
            for target in range(chips - 1, 0, -1):
                rs_up(part, target).start()

        @pl.when(z == chips - 1)
        def _():
            for target in range(chips - 1):
                rs_down(part, target).start()

    def rs_add(part, target):
        d_part[part, target] = (
            d_part[part, target].astype(jnp.float32) + d_recv[part, target].astype(jnp.float32)
        ).astype(jnp.bfloat16)

    def rs_slot(part, step):
        @pl.when((z >= 1) & (step >= z))
        def _():
            target = chips - 1 - step + z
            rs_arrived(part, target)

            @pl.when(target > z)
            def _():
                rs_add(part, target)
                rs_up(part, target).start()

        @pl.when((z < chips - 1) & (step >= chips - 1 - z))
        def _():
            target = step - (chips - 1) + z
            rs_arrived(part, jnp.where(target == z, chips, target))

            @pl.when(target < z)
            def _():
                rs_add(part, target)
                rs_down(part, target).start()

    def rs_finish(part):
        dq_ref[pl.ds(part * rows, rows), :] = d_part[part, z].astype(jnp.float32)

        @pl.when(z > 0)
        def _():
            dq_ref[pl.ds(part * rows, rows), :] += d_recv[part, z].astype(jnp.float32)

        @pl.when(z < chips - 1)
        def _():
            dq_ref[pl.ds(part * rows, rows), :] += d_recv[part, chips].astype(jnp.float32)

        for low in range(part * rows, (part + 1) * rows, strip):
            at = pl.ds(low, strip)
            dq_ref[at, :] = unit_back(inv_temp * dq_ref[at, :], q_ref[at, :])

    def rs_drain(part):
        for target in range(chips):
            @pl.when(z != target)
            def _():
                rs_up(part, target).wait_send()

    def tot_copy(part, off):
        return remote(totals.at[part, z], totals.at[part, z], tot_s.at[part, off],
                      tot_r.at[part, z], at_chip(peer_chip(off)))

    def code_copy(off):
        return remote(code_ref, codes.at[z], code_s.at[off], code_r.at[z],
                      at_chip(peer_chip(off)))

    def pass_copy(off):
        return remote(p_all.at[loop], p_all.at[loop], p_s.at[off], p_r.at[loop],
                      (peer_loop(off), me))

    def query_copy(part, off):
        return remote(q_all.at[part, z], q_loop.at[loop, part], ql_s.at[part, off],
                      ql_r.at[part, loop], (peer_loop(off), me))

    def coef_copy(off):
        to = peer_loop(off)
        return remote(c_part.at[to], c_recv.at[loop], c_s.at[off], c_r.at[loop], (to, me))

    pool_copy = remote(n_own, n_sib, sib_s.at[0], sib_r.at[0], (loop, sib))
    dn_copy = remote(dn_part, dn_recv, sib_s.at[1], sib_r.at[1], (loop, sib))

    def q_cols(part, cols):
        return q_all[part, :, :, cols].reshape(lanes, tile)

    def p_cols(cols):
        return p_all[:, :, cols].reshape(passages, tile)

    def columns(i):
        return pl.ds(pl.multiple_of(i * tile, tile), tile)

    ag_own(0)
    for off in range(1, chips):
        code_copy(off).start()

    @pl.loop(0, n_pass // strip)
    def _(i):
        at = pl.ds(pl.multiple_of(i * strip, strip), strip)
        p_all[loop, at, :] = unit_strip(p_ref[at, :])

    for off in range(1, loops):
        pass_copy(off).start()
    unit_queries(1)
    codes[z] = code_ref[...]
    ag_slot(0, 1)
    ag_own(1)

    @pl.loop(0, n_pool // strip)
    def _(i):
        at = pl.ds(pl.multiple_of(i * strip, strip), strip)
        n_own[at, :] = unit_strip(n_ref[at, :])

    pool_copy.start()
    for part in range(2, parts):
        unit_queries(part)
    for step in range(2, chips):
        ag_slot(0, step)
    for part in range(parts):
        q_loop[loop, part] = q_all[part, z]
    for off in range(1, chips):
        chip = peer_chip(off)
        remote(code_ref, codes.at[chip], code_s.at[off], code_r.at[chip],
               at_chip(chip)).wait_recv()
    pool_copy.wait_recv()
    for off in range(1, loops):
        other = peer_loop(off)
        remote(p_all.at[other], p_all.at[other], p_s.at[off], p_r.at[other],
               (other, me)).wait_recv()

    own_lane = lax.broadcasted_iota(jnp.int32, (1, lanes), 1) // rows == z
    top, bottom, end = n_pool, 2 * n_pool, 2 * n_pool + passages
    c_sum = jnp.zeros((passages, n_query), jnp.float32)

    for part in range(parts):
        def add_scores(i, carry):
            cols = columns(i)
            q_tile = q_cols(part, cols)
            return (
                carry[0] + cross(n_own[:, cols], q_tile),
                carry[1] + cross(n_sib[:, cols], q_tile),
                carry[2] + cross(p_cols(cols), q_tile),
            )

        s_own, s_sib, s_in = lax.fori_loop(
            0, tiles, add_scores,
            (jnp.zeros((n_pool, lanes), jnp.float32), jnp.zeros((n_pool, lanes), jnp.float32),
             jnp.zeros((passages, lanes), jnp.float32)),
        )
        part_codes = codes[0, part]
        for chip in range(1, chips):
            here = lax.broadcasted_iota(jnp.int32, part_codes.shape, 1) // rows == chip
            part_codes = jnp.where(here, codes[chip, part], part_codes)
        row_id = lax.broadcasted_iota(jnp.int32, (n_pool, lanes), 0)
        for first, owner, score in ((0, me, s_own), (top, sib, s_sib)):
            ids = row_id + owner * n_pool
            count = jnp.zeros((n_pool, lanes), jnp.float32)
            for k in range(part_codes.shape[0]):
                count += jnp.where(part_codes[k:k + 1, :] == ids, 1.0, 0.0)
            weights[0, first:first + n_pool, :] = count
            weights[1, first:first + n_pool, :] = jnp.exp(score * inv_temp - inv_temp)
        s_in = s_in * inv_temp
        weights[1, bottom:end, :] = jnp.exp(s_in - inv_temp)
        target = lax.broadcasted_iota(jnp.int32, (passages, lanes), 0) == pos_ref[part, 0:1, :]
        chosen = jnp.sum(jnp.where(target, s_in, 0.0), axis=0, keepdims=True)
        in_total = jnp.sum(weights[1, bottom:end, :], axis=0, keepdims=True)
        hard_total = jnp.sum(weights[0, 0:bottom, :] * weights[1, 0:bottom, :], axis=0,
                             keepdims=True)
        mine = hard_total + jnp.where(own_lane, in_total, 0.0)
        totals[part, z] = jnp.broadcast_to(mine, (8, lanes))
        for off in range(1, chips):
            tot_copy(part, off).start()

        for off in range(1, loops):
            query_copy(part, off).start()
        if part >= 1:
            rs_slot(part - 1, 1)
        if part + 1 < parts:
            ag_slot(part + 1, 1)
        if part >= 1 and chips > 2:
            rs_slot(part - 1, 2)

        for off in range(1, chips):
            chip = peer_chip(off)
            remote(totals.at[part, z], totals.at[part, chip], tot_s.at[part, off],
                   tot_r.at[part, chip], at_chip(chip)).wait_recv()
        total = totals[part, 0, 0:1, :]
        for chip in range(1, chips):
            total = total + totals[part, chip, 0:1, :]
        live = live_ref[part, 0:1, :]
        loss_ref[part] = jnp.broadcast_to(
            jnp.where(own_lane, live * (jnp.log(total) + inv_temp - chosen), 0.0), (8, lanes)
        )
        share = weights[1, 0:bottom, :] / total
        share = share.astype(jnp.bfloat16).astype(jnp.float32) * weights[0, 0:bottom, :]
        inside = weights[1, bottom:end, :] / total - jnp.where(target, 1.0, 0.0)
        inside = jnp.where(own_lane, live * inside, 0.0)
        place = pl.ds(part * lanes, lanes)
        coef[0:bottom, place] = share.astype(jnp.bfloat16)
        pick = lax.broadcasted_iota(jnp.int32, (lanes, n_query), 0) % rows + part * rows
        pick = jnp.where(pick == lax.broadcasted_iota(jnp.int32, (lanes, n_query), 1), 1.0, 0.0)
        c_sum = c_sum + plain(inside.astype(jnp.bfloat16), pick.astype(jnp.bfloat16))
        back = jnp.transpose(share).astype(jnp.bfloat16)
        back_in = jnp.transpose(inside).astype(jnp.bfloat16)

        @pl.loop(0, tiles)
        def _(i):
            cols = columns(i)
            grad = plain(back[:, 0:top], n_own[:, cols])
            grad += plain(back[:, top:bottom], n_sib[:, cols])
            grad += plain(back_in, p_cols(cols))
            d_part[part, :, :, cols] = grad.astype(jnp.bfloat16).reshape(chips, rows, tile)

        rs_start(part)
        if part + 2 < parts:
            ag_own(part + 2)
        if part >= 1:
            for step in range(3, chips):
                rs_slot(part - 1, step)
        if part + 1 < parts:
            for step in range(2, chips):
                ag_slot(part + 1, step)

    def q_whole(cols):
        return q_all[:, :, :, cols].reshape(parts * lanes, tile)

    c_part[...] = c_sum.astype(jnp.bfloat16).reshape(loops, n_pass, n_query)
    c_recv[loop] = c_part[loop]
    for off in range(1, loops):
        coef_copy(off).start()

    @pl.loop(0, tiles)
    def _(i):
        cols = columns(i)
        dn_part[:, cols] = plain(coef[top:bottom, :], q_whole(cols)).astype(jnp.bfloat16)

    dn_copy.start()
    rs_slot(parts - 1, 1)

    @pl.loop(0, tiles)
    def _(i):
        cols = columns(i)
        dn_ref[:, cols] = plain(coef[0:top, :], q_whole(cols))

    if chips > 2:
        rs_slot(parts - 1, 2)
    for part in range(parts - 1):
        rs_finish(part)
    for off in range(1, loops):
        other = peer_loop(off)
        remote(c_part.at[other], c_recv.at[other], c_s.at[off], c_r.at[other],
               (other, me)).wait_recv()
        for part in range(parts):
            remote(q_all.at[part, z], q_loop.at[other, part], ql_s.at[part, off],
                   ql_r.at[part, other], (other, me)).wait_recv()

    @pl.loop(0, tiles)
    def _(i):
        cols = columns(i)
        grad = jnp.zeros((n_pass, tile), jnp.float32)
        for other in range(loops):
            grad += plain(c_recv[other], q_loop[other, :, :, cols].reshape(n_query, tile))
        dp_ref[:, cols] = inv_temp * grad

    @pl.loop(0, n_pass // strip)
    def _(i):
        at = pl.ds(pl.multiple_of(i * strip, strip), strip)
        dp_ref[at, :] = unit_back(dp_ref[at, :], p_ref[at, :])

    dn_copy.wait_recv()

    @pl.loop(0, n_pool // strip)
    def _(i):
        at = pl.ds(pl.multiple_of(i * strip, strip), strip)
        grad = inv_temp * (dn_ref[at, :] + dn_recv[at, :].astype(jnp.float32))
        dn_ref[at, :] = unit_back(grad, n_ref[at, :])

    for step in range(3, chips):
        rs_slot(parts - 1, step)
    rs_finish(parts - 1)

    for part in range(parts):
        ag_drain(part)
        rs_drain(part)
        for off in range(1, chips):
            tot_copy(part, off).wait_send()
    for off in range(1, chips):
        code_copy(off).wait_send()
    for off in range(1, loops):
        pass_copy(off).wait_send()
        coef_copy(off).wait_send()
        for part in range(parts):
            query_copy(part, off).wait_send()
    pool_copy.wait_send()
    dn_copy.wait_send()


def local(queries, passages, pool, query_count, positive, neg_owner, neg_row):
    n_query, width = queries.shape
    n_pass = passages.shape[0]
    n_pool = pool.shape[0]
    hard_count = neg_owner.shape[1]
    loops = lax.axis_size("loop")
    chips = lax.axis_size("grp") // 2
    rows = n_query // parts
    lanes = chips * rows
    valid = lax.iota(jnp.int32, n_query) < query_count.reshape(())

    def spread(flat):
        cut = jnp.transpose(flat.reshape(parts, rows, -1), (0, 2, 1))
        return jnp.tile(cut, (1, 1, chips))

    wanted = jnp.where(valid[:, None], neg_owner * n_pool + neg_row, -1)
    wanted = jnp.pad(wanted, ((0, 0), (0, -hard_count % 8)), constant_values=-1)
    wanted = spread(wanted)
    pos = jnp.broadcast_to(spread(positive[:, None]), (parts, 8, lanes))
    live = jnp.broadcast_to(spread(valid.astype(jnp.float32)[:, None]), (parts, 8, lanes))
    vmem = pl.BlockSpec(memory_space=pltpu.VMEM)
    dma = pltpu.SemaphoreType.DMA
    bf16, f32 = jnp.bfloat16, jnp.float32
    all_rows = 2 * n_pool + loops * n_pass
    loss, grad_query, grad_passage, grad_pool = pl.pallas_call(
        functools.partial(kernel, loops, chips),
        out_shape=(
            jax.ShapeDtypeStruct((parts, 8, lanes), f32),
            jax.ShapeDtypeStruct((n_query, width), f32),
            jax.ShapeDtypeStruct((n_pass, width), f32),
            jax.ShapeDtypeStruct((n_pool, width), f32),
        ),
        in_specs=[vmem] * 6,
        out_specs=(vmem,) * 4,
        scratch_shapes=[
            pltpu.VMEM((parts, chips, rows, width), bf16),
            pltpu.VMEM((n_pool, width), bf16),
            pltpu.VMEM((n_pool, width), bf16),
            pltpu.VMEM((loops, n_pass, width), bf16),
            pltpu.VMEM((loops, parts, rows, width), bf16),
            pltpu.VMEM((chips,) + wanted.shape, jnp.int32),
            pltpu.VMEM((2, all_rows, lanes), f32),
            pltpu.VMEM((2 * n_pool, parts * lanes), bf16),
            pltpu.VMEM((parts, chips, 8, lanes), f32),
            pltpu.VMEM((parts, chips, rows, width), bf16),
            pltpu.VMEM((parts, chips + 1, rows, width), bf16),
            pltpu.VMEM((loops, n_pass, n_query), bf16),
            pltpu.VMEM((loops, n_pass, n_query), bf16),
            pltpu.VMEM((n_pool, width), bf16),
            pltpu.VMEM((n_pool, width), bf16),
            dma((parts, chips, 2)),
            dma((parts, chips)),
            dma((parts, chips)),
            dma((parts, chips + 1)),
            dma((parts, chips)),
            dma((parts, chips)),
            dma((chips,)),
            dma((chips,)),
            dma((loops,)),
            dma((loops,)),
            dma((parts, loops)),
            dma((parts, loops)),
            dma((loops,)),
            dma((loops,)),
            dma((2,)),
            dma((2,)),
        ],
        compiler_params=pltpu.CompilerParams(
            collective_id=0, has_side_effects=True, vmem_limit_bytes=63 * 1024 * 1024
        ),
    )(queries, passages, pool, wanted, pos, live)
    loss = jnp.sum(loss[:, 0, :].reshape(parts, chips, rows), axis=1).reshape(n_query)
    return (loss, grad_query, grad_passage, grad_pool)


def solution(mesh):
    return jax.shard_map(
        local,
        mesh=mesh,
        in_specs=(
            P(("loop", "grp"), None),
            P(("loop", "grp"), None),
            P(("loop", "grp"), None),
            P("loop", "grp"),
            P(("loop", "grp")),
            P(("loop", "grp"), None),
            P(("loop", "grp"), None),
        ),
        out_specs=(
            P(("loop", "grp")),
            P(("loop", "grp"), None),
            P(("loop", "grp"), None),
            P(("loop", "grp"), None),
        ),
        check_vma=False,
    )
```

```python
import functools

import jax
import jax.numpy as jnp
from jax import lax
from jax.experimental import pallas as pl
from jax.experimental.pallas import tpu as pltpu
from jax.sharding import PartitionSpec as P

inv_temp = 50.0
eps = 1e-06
parts = 8
ahead = 2
tile = 512
strip = 16


def scale_of(rows):
    return lax.rsqrt(jnp.sum(rows * rows, axis=-1, keepdims=True) + eps)


def unit_back(grad, raw):
    raw = raw.astype(jnp.float32)
    scale = scale_of(raw)
    unit = raw * scale
    return (grad - unit * jnp.sum(unit * grad, axis=-1, keepdims=True)) * scale


def cross(left, right):
    return lax.dot_general(
        left, right, (((1,), (1,)), ((), ())), preferred_element_type=jnp.float32
    )


def plain(left, right):
    return jnp.dot(left, right, preferred_element_type=jnp.float32)


def kernel(
    loops, chips, hard_count,
    q_ref, p_ref, n_ref, code_ref,
    loss_ref, dq_ref, dp_ref, dn_ref,
    q_all, n_own, n_sib, p_all, q_loop, codes, weights, coef, totals,
    d_part, d_recv, c_part, c_recv, dn_part, dn_recv,
    ag_s, ag_r, rs_s, rs_r, tot_s, tot_r, code_s, code_r,
    p_s, p_r, ql_s, ql_r, c_s, c_r, sib_s, sib_r,
):
    loop = lax.axis_index("loop")
    me = lax.axis_index("grp")
    z = me // 2
    core = me % 2
    sib = z * 2 + 1 - core
    n_query, width = q_ref.shape
    n_pass = p_ref.shape[0]
    n_pool = n_ref.shape[0]
    rows = n_query // parts
    lanes = chips * rows
    passages = loops * n_pass
    tiles = width // tile

    def at_chip(chip):
        return (loop, chip * 2 + core)

    def peer_chip(off):
        return lax.rem(z + off, chips)

    def peer_loop(off):
        return lax.rem(loop + off, loops)

    def remote(src, dst, send, recv, device):
        return pltpu.make_async_remote_copy(
            src_ref=src, dst_ref=dst, send_sem=send, recv_sem=recv,
            device_id=device, device_id_type=pl.DeviceIdType.MESH,
        )

    barrier = pltpu.get_barrier_semaphore()
    for off in range(1, chips):
        pl.semaphore_signal(barrier, inc=1, device_id=at_chip(peer_chip(off)),
                            device_id_type=pl.DeviceIdType.MESH)
    for off in range(1, loops):
        pl.semaphore_signal(barrier, inc=1, device_id=(peer_loop(off), me),
                            device_id_type=pl.DeviceIdType.MESH)
    pl.semaphore_signal(barrier, inc=1, device_id=(loop, sib),
                        device_id_type=pl.DeviceIdType.MESH)

    def unit_strip(raw):
        raw = raw.astype(jnp.float32)
        return (raw * scale_of(raw)).astype(jnp.bfloat16)

    def unit_queries(part):
        for low in range(0, rows, strip):
            q_all[part, z, low:low + strip, :] = unit_strip(
                q_ref[part * rows + low:part * rows + low + strip, :])

    unit_queries(0)
    pl.semaphore_wait(barrier, chips + loops - 1)

    def ag_copy(part, block, up):
        way = 0 if up else 1
        chip = z + 1 if up else z - 1
        return remote(q_all.at[part, block], q_all.at[part, block], ag_s.at[part, block, way],
                      ag_r.at[part, block], at_chip(chip))

    def ag_own(part):
        @pl.when((z < chips - 1) & (z > 0))
        def _():
            ag_copy(part, z, True).start()
            ag_copy(part, z, False).start()

    def ag_ends(part):
        @pl.when(z == 0)
        def _():
            ag_copy(part, z, True).start()

        @pl.when(z == chips - 1)
        def _():
            ag_copy(part, z, False).start()

    def ag_slot(part, step):
        @pl.when(z - step >= 0)
        def _():
            ag_copy(part, z - step, True).wait_recv()

            @pl.when(z < chips - 1)
            def _():
                ag_copy(part, z - step, True).start()

        @pl.when(z + step < chips)
        def _():
            ag_copy(part, z + step, False).wait_recv()

            @pl.when(z > 0)
            def _():
                ag_copy(part, z + step, False).start()

    def ag_drain(part):
        for step in range(chips):
            @pl.when((z - step >= 0) & (z < chips - 1))
            def _():
                ag_copy(part, z - step, True).wait_send()

            @pl.when((z + step < chips) & (z > 0))
            def _():
                ag_copy(part, z + step, False).wait_send()

    def rs_up(part, target):
        return remote(d_part.at[part, target], d_recv.at[part, target],
                      rs_s.at[part, target], rs_r.at[part, target], at_chip(z + 1))

    def rs_down(part, target):
        slot = jnp.where(target == z - 1, chips, target)
        return remote(d_part.at[part, target], d_recv.at[part, slot],
                      rs_s.at[part, target], rs_r.at[part, slot], at_chip(z - 1))

    def rs_arrived(part, slot):
        remote(d_part.at[part, 0], d_recv.at[part, slot],
               rs_s.at[part, 0], rs_r.at[part, slot], at_chip(z)).wait_recv()

    def rs_start(part):
        @pl.when(z == 0)
        def _():
            for target in range(chips - 1, 0, -1):
                rs_up(part, target).start()

        @pl.when(z == chips - 1)
        def _():
            for target in range(chips - 1):
                rs_down(part, target).start()

    def rs_add(part, target):
        d_part[part, target] = (
            d_part[part, target].astype(jnp.float32) + d_recv[part, target].astype(jnp.float32)
        ).astype(jnp.bfloat16)

    def rs_slot(part, step):
        @pl.when((z >= 1) & (step >= z))
        def _():
            target = chips - 1 - step + z
            rs_arrived(part, target)

            @pl.when(target > z)
            def _():
                rs_add(part, target)
                rs_up(part, target).start()

        @pl.when((z < chips - 1) & (step >= chips - 1 - z))
        def _():
            target = step - (chips - 1) + z
            rs_arrived(part, jnp.where(target == z, chips, target))

            @pl.when(target < z)
            def _():
                rs_add(part, target)
                rs_down(part, target).start()

    def rs_finish(part):
        dq_ref[pl.ds(part * rows, rows), :] = d_part[part, z].astype(jnp.float32)

        @pl.when(z > 0)
        def _():
            dq_ref[pl.ds(part * rows, rows), :] += d_recv[part, z].astype(jnp.float32)

        @pl.when(z < chips - 1)
        def _():
            dq_ref[pl.ds(part * rows, rows), :] += d_recv[part, chips].astype(jnp.float32)

        for low in range(part * rows, (part + 1) * rows, strip):
            at = pl.ds(low, strip)
            dq_ref[at, :] = unit_back(inv_temp * dq_ref[at, :], q_ref[at, :])

    def rs_drain(part):
        for target in range(chips):
            @pl.when(z != target)
            def _():
                rs_up(part, target).wait_send()

    def tot_copy(part, off):
        return remote(totals.at[part, z], totals.at[part, z], tot_s.at[part, off],
                      tot_r.at[part, z], at_chip(peer_chip(off)))

    def code_copy(off):
        return remote(code_ref, codes.at[z], code_s.at[off], code_r.at[z],
                      at_chip(peer_chip(off)))

    def pass_copy(off):
        return remote(p_all.at[loop], p_all.at[loop], p_s.at[off], p_r.at[loop],
                      (peer_loop(off), me))

    def query_copy(part, off):
        return remote(q_all.at[part, z], q_loop.at[loop, part], ql_s.at[part, off],
                      ql_r.at[part, loop], (peer_loop(off), me))

    def coef_copy(off):
        to = peer_loop(off)
        return remote(c_part.at[to], c_recv.at[loop], c_s.at[off], c_r.at[loop], (to, me))

    pool_copy = remote(n_own, n_sib, sib_s.at[0], sib_r.at[0], (loop, sib))
    dn_copy = remote(dn_part, dn_recv, sib_s.at[1], sib_r.at[1], (loop, sib))

    def q_cols(part, cols):
        return q_all[part, :, :, cols].reshape(lanes, tile)

    def p_cols(cols):
        return p_all[:, :, cols].reshape(passages, tile)

    def columns(i):
        return pl.ds(pl.multiple_of(i * tile, tile), tile)

    ag_own(0)
    ag_ends(0)
    for off in range(1, chips):
        code_copy(off).start()

    @pl.loop(0, n_pass // strip)
    def _(i):
        at = pl.ds(pl.multiple_of(i * strip, strip), strip)
        p_all[loop, at, :] = unit_strip(p_ref[at, :])

    for off in range(1, loops):
        pass_copy(off).start()
    unit_queries(1)
    codes[z] = code_ref[...]
    ag_ends(1)
    ag_slot(0, 1)
    ag_own(1)
    for part in range(2, parts):
        unit_queries(part)
        ag_ends(part)
    for step in range(2, chips):
        ag_slot(0, step)

    @pl.loop(0, n_pool // strip)
    def _(i):
        at = pl.ds(pl.multiple_of(i * strip, strip), strip)
        n_own[at, :] = unit_strip(n_ref[at, :])

    pool_copy.start()
    for part in range(1, ahead):
        ag_slot(part, 1)
        ag_own(part + 1)
        for step in range(2, chips):
            ag_slot(part, step)
    for part in range(parts):
        q_loop[loop, part] = q_all[part, z]
    for off in range(1, chips):
        chip = peer_chip(off)
        remote(code_ref, codes.at[chip], code_s.at[off], code_r.at[chip],
               at_chip(chip)).wait_recv()
    pool_copy.wait_recv()
    for off in range(1, loops):
        other = peer_loop(off)
        remote(p_all.at[other], p_all.at[other], p_s.at[off], p_r.at[other],
               (other, me)).wait_recv()

    own_lane = lax.broadcasted_iota(jnp.int32, (1, lanes), 1) // rows == z
    top, bottom, end = n_pool, 2 * n_pool, 2 * n_pool + passages
    c_sum = jnp.zeros((passages, n_query), jnp.float32)

    for part in range(parts):
        def add_scores(i, carry):
            cols = columns(i)
            q_tile = q_cols(part, cols)
            return (
                carry[0] + cross(n_own[:, cols], q_tile),
                carry[1] + cross(n_sib[:, cols], q_tile),
                carry[2] + cross(p_cols(cols), q_tile),
            )

        s_own, s_sib, s_in = lax.fori_loop(
            0, tiles, add_scores,
            (jnp.zeros((n_pool, lanes), jnp.float32), jnp.zeros((n_pool, lanes), jnp.float32),
             jnp.zeros((passages, lanes), jnp.float32)),
        )
        part_codes = codes[0, part]
        for chip in range(1, chips):
            here = lax.broadcasted_iota(jnp.int32, part_codes.shape, 1) // rows == chip
            part_codes = jnp.where(here, codes[chip, part], part_codes)
        row_id = lax.broadcasted_iota(jnp.int32, (n_pool, lanes), 0)
        for first, owner, score in ((0, me, s_own), (top, sib, s_sib)):
            ids = row_id + owner * n_pool
            count = jnp.zeros((n_pool, lanes), jnp.float32)
            for k in range(hard_count):
                count += jnp.where(part_codes[k:k + 1, :] == ids, 1.0, 0.0)
            weights[0, first:first + n_pool, :] = count
            weights[1, first:first + n_pool, :] = jnp.exp(score * inv_temp - inv_temp)
        s_in = s_in * inv_temp
        positive = code_ref[part, hard_count:hard_count + 1, :]
        weights[1, bottom:end, :] = jnp.exp(s_in - inv_temp)
        target = lax.broadcasted_iota(jnp.int32, (passages, lanes), 0) == positive
        chosen = jnp.sum(jnp.where(target, s_in, 0.0), axis=0, keepdims=True)
        in_total = jnp.sum(weights[1, bottom:end, :], axis=0, keepdims=True)
        hard_total = jnp.sum(weights[0, 0:bottom, :] * weights[1, 0:bottom, :], axis=0,
                             keepdims=True)
        mine = hard_total + jnp.where(own_lane, in_total, 0.0)
        totals[part, z] = jnp.broadcast_to(mine, (8, lanes))
        for off in range(1, chips):
            tot_copy(part, off).start()

        for off in range(1, loops):
            query_copy(part, off).start()
        if part >= 1:
            rs_slot(part - 1, 1)
        if part + ahead < parts:
            ag_slot(part + ahead, 1)
        if part >= 1 and chips > 2:
            rs_slot(part - 1, 2)

        for off in range(1, chips):
            chip = peer_chip(off)
            remote(totals.at[part, z], totals.at[part, chip], tot_s.at[part, off],
                   tot_r.at[part, chip], at_chip(chip)).wait_recv()
        total = totals[part, 0, 0:1, :]
        for chip in range(1, chips):
            total = total + totals[part, chip, 0:1, :]
        live = jnp.where(positive >= 0, 1.0, 0.0)
        loss_ref[part] = jnp.broadcast_to(
            jnp.where(own_lane, live * (jnp.log(total) + inv_temp - chosen), 0.0), (8, lanes)
        )
        share = weights[1, 0:bottom, :] / total
        share = share.astype(jnp.bfloat16).astype(jnp.float32) * weights[0, 0:bottom, :]
        inside = weights[1, bottom:end, :] / total - jnp.where(target, 1.0, 0.0)
        inside = jnp.where(own_lane, live * inside, 0.0)
        place = pl.ds(part * lanes, lanes)
        coef[0:bottom, place] = share.astype(jnp.bfloat16)
        pick = lax.broadcasted_iota(jnp.int32, (lanes, n_query), 0) % rows + part * rows
        pick = jnp.where(pick == lax.broadcasted_iota(jnp.int32, (lanes, n_query), 1), 1.0, 0.0)
        c_sum = c_sum + plain(inside.astype(jnp.bfloat16), pick.astype(jnp.bfloat16))
        back = jnp.transpose(share).astype(jnp.bfloat16)
        back_in = jnp.transpose(inside).astype(jnp.bfloat16)

        @pl.loop(0, tiles)
        def _(i):
            cols = columns(i)
            grad = plain(back[:, 0:top], n_own[:, cols])
            grad += plain(back[:, top:bottom], n_sib[:, cols])
            grad += plain(back_in, p_cols(cols))
            d_part[part, :, :, cols] = grad.astype(jnp.bfloat16).reshape(chips, rows, tile)

        rs_start(part)
        if part + ahead + 1 < parts:
            ag_own(part + ahead + 1)
        if part >= 1:
            for step in range(3, chips):
                rs_slot(part - 1, step)
        if part + ahead < parts:
            for step in range(2, chips):
                ag_slot(part + ahead, step)

    def q_whole(cols):
        return q_all[:, :, :, cols].reshape(parts * lanes, tile)

    c_part[...] = c_sum.astype(jnp.bfloat16).reshape(loops, n_pass, n_query)
    c_recv[loop] = c_part[loop]
    for off in range(1, loops):
        coef_copy(off).start()

    @pl.loop(0, tiles)
    def _(i):
        cols = columns(i)
        dn_part[:, cols] = plain(coef[top:bottom, :], q_whole(cols)).astype(jnp.bfloat16)

    dn_copy.start()
    rs_slot(parts - 1, 1)

    @pl.loop(0, tiles)
    def _(i):
        cols = columns(i)
        dn_ref[:, cols] = plain(coef[0:top, :], q_whole(cols))

    if chips > 2:
        rs_slot(parts - 1, 2)
    for part in range(parts - 1):
        rs_finish(part)
    for off in range(1, loops):
        other = peer_loop(off)
        remote(c_part.at[other], c_recv.at[other], c_s.at[off], c_r.at[other],
               (other, me)).wait_recv()
        for part in range(parts):
            remote(q_all.at[part, z], q_loop.at[other, part], ql_s.at[part, off],
                   ql_r.at[part, other], (other, me)).wait_recv()

    @pl.loop(0, tiles)
    def _(i):
        cols = columns(i)
        grad = jnp.zeros((n_pass, tile), jnp.float32)
        for other in range(loops):
            grad += plain(c_recv[other], q_loop[other, :, :, cols].reshape(n_query, tile))
        dp_ref[:, cols] = inv_temp * grad

    @pl.loop(0, n_pass // strip)
    def _(i):
        at = pl.ds(pl.multiple_of(i * strip, strip), strip)
        dp_ref[at, :] = unit_back(dp_ref[at, :], p_ref[at, :])

    dn_copy.wait_recv()

    @pl.loop(0, n_pool // strip)
    def _(i):
        at = pl.ds(pl.multiple_of(i * strip, strip), strip)
        grad = inv_temp * (dn_ref[at, :] + dn_recv[at, :].astype(jnp.float32))
        dn_ref[at, :] = unit_back(grad, n_ref[at, :])

    for step in range(3, chips):
        rs_slot(parts - 1, step)
    rs_finish(parts - 1)

    for part in range(parts):
        ag_drain(part)
        rs_drain(part)
        for off in range(1, chips):
            tot_copy(part, off).wait_send()
    for off in range(1, chips):
        code_copy(off).wait_send()
    for off in range(1, loops):
        pass_copy(off).wait_send()
        coef_copy(off).wait_send()
        for part in range(parts):
            query_copy(part, off).wait_send()
    pool_copy.wait_send()
    dn_copy.wait_send()


def local(queries, passages, pool, query_count, positive, neg_owner, neg_row):
    n_query, width = queries.shape
    n_pass = passages.shape[0]
    n_pool = pool.shape[0]
    hard_count = neg_owner.shape[1]
    loops = lax.axis_size("loop")
    chips = lax.axis_size("grp") // 2
    rows = n_query // parts
    lanes = chips * rows
    valid = lax.iota(jnp.int32, n_query) < query_count.reshape(())

    wanted = jnp.concatenate([neg_owner * n_pool + neg_row, positive[:, None]], axis=1)
    wanted = jnp.where(valid[:, None], wanted, -1)
    wanted = jnp.pad(wanted, ((0, 0), (0, -(hard_count + 1) % 8)), constant_values=-1)
    wanted = jnp.transpose(wanted.reshape(parts, rows, -1), (0, 2, 1))
    wanted = jnp.tile(wanted, (1, 1, chips))
    vmem = pl.BlockSpec(memory_space=pltpu.VMEM)
    dma = pltpu.SemaphoreType.DMA
    bf16, f32 = jnp.bfloat16, jnp.float32
    all_rows = 2 * n_pool + loops * n_pass
    loss, grad_query, grad_passage, grad_pool = pl.pallas_call(
        functools.partial(kernel, loops, chips, hard_count),
        out_shape=(
            jax.ShapeDtypeStruct((parts, 8, lanes), f32),
            jax.ShapeDtypeStruct((n_query, width), f32),
            jax.ShapeDtypeStruct((n_pass, width), f32),
            jax.ShapeDtypeStruct((n_pool, width), f32),
        ),
        in_specs=[vmem] * 4,
        out_specs=(vmem,) * 4,
        scratch_shapes=[
            pltpu.VMEM((parts, chips, rows, width), bf16),
            pltpu.VMEM((n_pool, width), bf16),
            pltpu.VMEM((n_pool, width), bf16),
            pltpu.VMEM((loops, n_pass, width), bf16),
            pltpu.VMEM((loops, parts, rows, width), bf16),
            pltpu.VMEM((chips,) + wanted.shape, jnp.int32),
            pltpu.VMEM((2, all_rows, lanes), f32),
            pltpu.VMEM((2 * n_pool, parts * lanes), bf16),
            pltpu.VMEM((parts, chips, 8, lanes), f32),
            pltpu.VMEM((parts, chips, rows, width), bf16),
            pltpu.VMEM((parts, chips + 1, rows, width), bf16),
            pltpu.VMEM((loops, n_pass, n_query), bf16),
            pltpu.VMEM((loops, n_pass, n_query), bf16),
            pltpu.VMEM((n_pool, width), bf16),
            pltpu.VMEM((n_pool, width), bf16),
            dma((parts, chips, 2)),
            dma((parts, chips)),
            dma((parts, chips)),
            dma((parts, chips + 1)),
            dma((parts, chips)),
            dma((parts, chips)),
            dma((chips,)),
            dma((chips,)),
            dma((loops,)),
            dma((loops,)),
            dma((parts, loops)),
            dma((parts, loops)),
            dma((loops,)),
            dma((loops,)),
            dma((2,)),
            dma((2,)),
        ],
        compiler_params=pltpu.CompilerParams(
            collective_id=0, has_side_effects=True, vmem_limit_bytes=63 * 1024 * 1024
        ),
    )(queries, passages, pool, wanted)
    loss = jnp.sum(loss[:, 0, :].reshape(parts, chips, rows), axis=1).reshape(n_query)
    return (loss, grad_query, grad_passage, grad_pool)


def solution(mesh):
    return jax.shard_map(
        local,
        mesh=mesh,
        in_specs=(
            P(("loop", "grp"), None),
            P(("loop", "grp"), None),
            P(("loop", "grp"), None),
            P("loop", "grp"),
            P(("loop", "grp")),
            P(("loop", "grp"), None),
            P(("loop", "grp"), None),
        ),
        out_specs=(
            P(("loop", "grp")),
            P(("loop", "grp"), None),
            P(("loop", "grp"), None),
            P(("loop", "grp"), None),
        ),
        check_vma=False,
    )
```

```python
import functools

import jax
import jax.numpy as jnp
from jax import lax
from jax.experimental import pallas as pl
from jax.experimental.pallas import tpu as pltpu
from jax.sharding import PartitionSpec as P

inv_temp = 50.0
eps = 1e-06
parts = 4
ahead = 1
tile = 1024
strip = 16


def scale_of(rows):
    return lax.rsqrt(jnp.sum(rows * rows, axis=-1, keepdims=True) + eps)


def unit_back(grad, raw):
    raw = raw.astype(jnp.float32)
    scale = scale_of(raw)
    unit = raw * scale
    return (grad - unit * jnp.sum(unit * grad, axis=-1, keepdims=True)) * scale


def cross(left, right):
    return lax.dot_general(
        left, right, (((1,), (1,)), ((), ())), preferred_element_type=jnp.float32
    )


def plain(left, right):
    return jnp.dot(left, right, preferred_element_type=jnp.float32)


def kernel(
    loops, chips, hard_count,
    q_ref, p_ref, n_ref, code_ref,
    loss_ref, dq_ref, dp_ref, dn_ref,
    q_all, n_own, n_sib, p_all, q_loop, codes, weights, coef, totals,
    d_part, d_recv, c_part, c_recv, dn_part, dn_recv,
    ag_s, ag_r, rs_s, rs_r, tot_s, tot_r, code_s, code_r,
    p_s, p_r, ql_s, ql_r, c_s, c_r, sib_s, sib_r,
):
    loop = lax.axis_index("loop")
    me = lax.axis_index("grp")
    z = me // 2
    core = me % 2
    sib = z * 2 + 1 - core
    n_query, width = q_ref.shape
    n_pass = p_ref.shape[0]
    n_pool = n_ref.shape[0]
    rows = n_query // parts
    lanes = chips * rows
    passages = loops * n_pass
    tiles = width // tile

    def at_chip(chip):
        return (loop, chip * 2 + core)

    def peer_chip(off):
        return lax.rem(z + off, chips)

    def peer_loop(off):
        return lax.rem(loop + off, loops)

    def remote(src, dst, send, recv, device):
        return pltpu.make_async_remote_copy(
            src_ref=src, dst_ref=dst, send_sem=send, recv_sem=recv,
            device_id=device, device_id_type=pl.DeviceIdType.MESH,
        )

    barrier = pltpu.get_barrier_semaphore()
    for off in range(1, chips):
        pl.semaphore_signal(barrier, inc=1, device_id=at_chip(peer_chip(off)),
                            device_id_type=pl.DeviceIdType.MESH)
    for off in range(1, loops):
        pl.semaphore_signal(barrier, inc=1, device_id=(peer_loop(off), me),
                            device_id_type=pl.DeviceIdType.MESH)
    pl.semaphore_signal(barrier, inc=1, device_id=(loop, sib),
                        device_id_type=pl.DeviceIdType.MESH)

    def unit_strip(raw):
        raw = raw.astype(jnp.float32)
        return (raw * scale_of(raw)).astype(jnp.bfloat16)

    def unit_queries(part):
        for low in range(0, rows, strip):
            q_all[part, z, low:low + strip, :] = unit_strip(
                q_ref[part * rows + low:part * rows + low + strip, :])

    unit_queries(0)
    pl.semaphore_wait(barrier, chips + loops - 1)

    def ag_copy(part, block, up):
        way = 0 if up else 1
        chip = z + 1 if up else z - 1
        return remote(q_all.at[part, block], q_all.at[part, block], ag_s.at[part, block, way],
                      ag_r.at[part, block], at_chip(chip))

    def ag_own(part):
        @pl.when((z < chips - 1) & (z > 0))
        def _():
            ag_copy(part, z, True).start()
            ag_copy(part, z, False).start()

    def ag_ends(part):
        @pl.when(z == 0)
        def _():
            ag_copy(part, z, True).start()

        @pl.when(z == chips - 1)
        def _():
            ag_copy(part, z, False).start()

    def ag_slot(part, step):
        @pl.when(z - step >= 0)
        def _():
            ag_copy(part, z - step, True).wait_recv()

            @pl.when(z < chips - 1)
            def _():
                ag_copy(part, z - step, True).start()

        @pl.when(z + step < chips)
        def _():
            ag_copy(part, z + step, False).wait_recv()

            @pl.when(z > 0)
            def _():
                ag_copy(part, z + step, False).start()

    def ag_drain(part):
        for step in range(chips):
            @pl.when((z - step >= 0) & (z < chips - 1))
            def _():
                ag_copy(part, z - step, True).wait_send()

            @pl.when((z + step < chips) & (z > 0))
            def _():
                ag_copy(part, z + step, False).wait_send()

    def rs_up(part, target):
        return remote(d_part.at[part, target], d_recv.at[part, target],
                      rs_s.at[part, target], rs_r.at[part, target], at_chip(z + 1))

    def rs_down(part, target):
        slot = jnp.where(target == z - 1, chips, target)
        return remote(d_part.at[part, target], d_recv.at[part, slot],
                      rs_s.at[part, target], rs_r.at[part, slot], at_chip(z - 1))

    def rs_arrived(part, slot):
        remote(d_part.at[part, 0], d_recv.at[part, slot],
               rs_s.at[part, 0], rs_r.at[part, slot], at_chip(z)).wait_recv()

    def rs_start(part):
        @pl.when(z == 0)
        def _():
            for target in range(chips - 1, 0, -1):
                rs_up(part, target).start()

        @pl.when(z == chips - 1)
        def _():
            for target in range(chips - 1):
                rs_down(part, target).start()

    def rs_add(part, target):
        d_part[part, target] = (
            d_part[part, target].astype(jnp.float32) + d_recv[part, target].astype(jnp.float32)
        ).astype(jnp.bfloat16)

    def rs_slot(part, step):
        @pl.when((z >= 1) & (step >= z))
        def _():
            target = chips - 1 - step + z
            rs_arrived(part, target)

            @pl.when(target > z)
            def _():
                rs_add(part, target)
                rs_up(part, target).start()

        @pl.when((z < chips - 1) & (step >= chips - 1 - z))
        def _():
            target = step - (chips - 1) + z
            rs_arrived(part, jnp.where(target == z, chips, target))

            @pl.when(target < z)
            def _():
                rs_add(part, target)
                rs_down(part, target).start()

    def rs_finish(part):
        dq_ref[pl.ds(part * rows, rows), :] = d_part[part, z].astype(jnp.float32)

        @pl.when(z > 0)
        def _():
            dq_ref[pl.ds(part * rows, rows), :] += d_recv[part, z].astype(jnp.float32)

        @pl.when(z < chips - 1)
        def _():
            dq_ref[pl.ds(part * rows, rows), :] += d_recv[part, chips].astype(jnp.float32)

        for low in range(part * rows, (part + 1) * rows, strip):
            at = pl.ds(low, strip)
            dq_ref[at, :] = unit_back(inv_temp * dq_ref[at, :], q_ref[at, :])

    def rs_drain(part):
        for target in range(chips):
            @pl.when(z != target)
            def _():
                rs_up(part, target).wait_send()

    def tot_copy(part, off):
        return remote(totals.at[part, z], totals.at[part, z], tot_s.at[part, off],
                      tot_r.at[part, z], at_chip(peer_chip(off)))

    def code_copy(off):
        return remote(code_ref, codes.at[z], code_s.at[off], code_r.at[z],
                      at_chip(peer_chip(off)))

    def pass_copy(off):
        return remote(p_all.at[loop], p_all.at[loop], p_s.at[off], p_r.at[loop],
                      (peer_loop(off), me))

    def query_copy(part, off):
        return remote(q_all.at[part, z], q_loop.at[loop, part], ql_s.at[part, off],
                      ql_r.at[part, loop], (peer_loop(off), me))

    def coef_copy(off):
        to = peer_loop(off)
        return remote(c_part.at[to], c_recv.at[loop], c_s.at[off], c_r.at[loop], (to, me))

    pool_copy = remote(n_own, n_sib, sib_s.at[0], sib_r.at[0], (loop, sib))
    dn_copy = remote(dn_part, dn_recv, sib_s.at[1], sib_r.at[1], (loop, sib))

    def q_cols(part, cols):
        return q_all[part, :, :, cols].reshape(lanes, tile)

    def p_cols(cols):
        return p_all[:, :, cols].reshape(passages, tile)

    def columns(i):
        return pl.ds(pl.multiple_of(i * tile, tile), tile)

    ag_own(0)
    ag_ends(0)
    for off in range(1, chips):
        code_copy(off).start()

    @pl.loop(0, n_pass // strip)
    def _(i):
        at = pl.ds(pl.multiple_of(i * strip, strip), strip)
        p_all[loop, at, :] = unit_strip(p_ref[at, :])

    for off in range(1, loops):
        pass_copy(off).start()
    unit_queries(1)
    codes[z] = code_ref[...]
    ag_ends(1)
    ag_slot(0, 1)
    ag_own(1)
    for part in range(2, parts):
        unit_queries(part)
        ag_ends(part)
    for step in range(2, chips):
        ag_slot(0, step)

    @pl.loop(0, n_pool // strip)
    def _(i):
        at = pl.ds(pl.multiple_of(i * strip, strip), strip)
        n_own[at, :] = unit_strip(n_ref[at, :])

    pool_copy.start()
    for part in range(1, ahead):
        ag_slot(part, 1)
        ag_own(part + 1)
        for step in range(2, chips):
            ag_slot(part, step)
    for part in range(parts):
        q_loop[loop, part] = q_all[part, z]
    for off in range(1, chips):
        chip = peer_chip(off)
        remote(code_ref, codes.at[chip], code_s.at[off], code_r.at[chip],
               at_chip(chip)).wait_recv()
    pool_copy.wait_recv()
    for off in range(1, loops):
        other = peer_loop(off)
        remote(p_all.at[other], p_all.at[other], p_s.at[off], p_r.at[other],
               (other, me)).wait_recv()

    own_lane = lax.broadcasted_iota(jnp.int32, (1, lanes), 1) // rows == z
    top, bottom, end = n_pool, 2 * n_pool, 2 * n_pool + passages
    c_sum = jnp.zeros((passages, n_query), jnp.float32)

    for part in range(parts):
        def add_scores(i, carry):
            cols = columns(i)
            q_tile = q_cols(part, cols)
            return (
                carry[0] + cross(n_own[:, cols], q_tile),
                carry[1] + cross(n_sib[:, cols], q_tile),
                carry[2] + cross(p_cols(cols), q_tile),
            )

        s_own, s_sib, s_in = lax.fori_loop(
            0, tiles, add_scores,
            (jnp.zeros((n_pool, lanes), jnp.float32), jnp.zeros((n_pool, lanes), jnp.float32),
             jnp.zeros((passages, lanes), jnp.float32)),
        )
        part_codes = codes[0, part]
        for chip in range(1, chips):
            here = lax.broadcasted_iota(jnp.int32, part_codes.shape, 1) // rows == chip
            part_codes = jnp.where(here, codes[chip, part], part_codes)
        row_id = lax.broadcasted_iota(jnp.int32, (n_pool, lanes), 0)
        for first, owner, score in ((0, me, s_own), (top, sib, s_sib)):
            ids = row_id + owner * n_pool
            count = jnp.zeros((n_pool, lanes), jnp.float32)
            for k in range(hard_count):
                count += jnp.where(part_codes[k:k + 1, :] == ids, 1.0, 0.0)
            weights[0, first:first + n_pool, :] = count
            weights[1, first:first + n_pool, :] = jnp.exp(score * inv_temp - inv_temp)
        s_in = s_in * inv_temp
        positive = code_ref[part, hard_count:hard_count + 1, :]
        weights[1, bottom:end, :] = jnp.exp(s_in - inv_temp)
        target = lax.broadcasted_iota(jnp.int32, (passages, lanes), 0) == positive
        chosen = jnp.sum(jnp.where(target, s_in, 0.0), axis=0, keepdims=True)
        in_total = jnp.sum(weights[1, bottom:end, :], axis=0, keepdims=True)
        hard_total = jnp.sum(weights[0, 0:bottom, :] * weights[1, 0:bottom, :], axis=0,
                             keepdims=True)
        mine = hard_total + jnp.where(own_lane, in_total, 0.0)
        totals[part, z] = jnp.broadcast_to(mine, (8, lanes))
        for off in range(1, chips):
            tot_copy(part, off).start()

        for off in range(1, loops):
            query_copy(part, off).start()
        if part >= 1:
            rs_slot(part - 1, 1)
        if part + ahead < parts:
            ag_slot(part + ahead, 1)
        if part >= 1 and chips > 2:
            rs_slot(part - 1, 2)

        for off in range(1, chips):
            chip = peer_chip(off)
            remote(totals.at[part, z], totals.at[part, chip], tot_s.at[part, off],
                   tot_r.at[part, chip], at_chip(chip)).wait_recv()
        total = totals[part, 0, 0:1, :]
        for chip in range(1, chips):
            total = total + totals[part, chip, 0:1, :]
        live = jnp.where(positive >= 0, 1.0, 0.0)
        loss_ref[part] = jnp.broadcast_to(
            jnp.where(own_lane, live * (jnp.log(total) + inv_temp - chosen), 0.0), (8, lanes)
        )
        share = weights[1, 0:bottom, :] / total
        share = share.astype(jnp.bfloat16).astype(jnp.float32) * weights[0, 0:bottom, :]
        inside = weights[1, bottom:end, :] / total - jnp.where(target, 1.0, 0.0)
        inside = jnp.where(own_lane, live * inside, 0.0)
        place = pl.ds(part * lanes, lanes)
        coef[0:bottom, place] = share.astype(jnp.bfloat16)
        pick = lax.broadcasted_iota(jnp.int32, (lanes, n_query), 0) % rows + part * rows
        pick = jnp.where(pick == lax.broadcasted_iota(jnp.int32, (lanes, n_query), 1), 1.0, 0.0)
        c_sum = c_sum + plain(inside.astype(jnp.bfloat16), pick.astype(jnp.bfloat16))
        back = jnp.transpose(share).astype(jnp.bfloat16)
        back_in = jnp.transpose(inside).astype(jnp.bfloat16)

        @pl.loop(0, tiles)
        def _(i):
            cols = columns(i)
            grad = plain(back[:, 0:top], n_own[:, cols])
            grad += plain(back[:, top:bottom], n_sib[:, cols])
            grad += plain(back_in, p_cols(cols))
            d_part[part, :, :, cols] = grad.astype(jnp.bfloat16).reshape(chips, rows, tile)

        rs_start(part)
        if part + ahead + 1 < parts:
            ag_own(part + ahead + 1)
        if part >= 1:
            for step in range(3, chips):
                rs_slot(part - 1, step)
        if part + ahead < parts:
            for step in range(2, chips):
                ag_slot(part + ahead, step)

    def q_whole(cols):
        return q_all[:, :, :, cols].reshape(parts * lanes, tile)

    c_part[...] = c_sum.astype(jnp.bfloat16).reshape(loops, n_pass, n_query)
    c_recv[loop] = c_part[loop]
    for off in range(1, loops):
        coef_copy(off).start()

    @pl.loop(0, tiles)
    def _(i):
        cols = columns(i)
        dn_part[:, cols] = plain(coef[top:bottom, :], q_whole(cols)).astype(jnp.bfloat16)

    dn_copy.start()
    rs_slot(parts - 1, 1)

    @pl.loop(0, tiles)
    def _(i):
        cols = columns(i)
        dn_ref[:, cols] = plain(coef[0:top, :], q_whole(cols))

    if chips > 2:
        rs_slot(parts - 1, 2)
    for part in range(parts - 1):
        rs_finish(part)
    for off in range(1, loops):
        other = peer_loop(off)
        remote(c_part.at[other], c_recv.at[other], c_s.at[off], c_r.at[other],
               (other, me)).wait_recv()
        for part in range(parts):
            remote(q_all.at[part, z], q_loop.at[other, part], ql_s.at[part, off],
                   ql_r.at[part, other], (other, me)).wait_recv()

    @pl.loop(0, tiles)
    def _(i):
        cols = columns(i)
        grad = jnp.zeros((n_pass, tile), jnp.float32)
        for other in range(loops):
            grad += plain(c_recv[other], q_loop[other, :, :, cols].reshape(n_query, tile))
        dp_ref[:, cols] = inv_temp * grad

    @pl.loop(0, n_pass // strip)
    def _(i):
        at = pl.ds(pl.multiple_of(i * strip, strip), strip)
        dp_ref[at, :] = unit_back(dp_ref[at, :], p_ref[at, :])

    dn_copy.wait_recv()

    @pl.loop(0, n_pool // strip)
    def _(i):
        at = pl.ds(pl.multiple_of(i * strip, strip), strip)
        grad = inv_temp * (dn_ref[at, :] + dn_recv[at, :].astype(jnp.float32))
        dn_ref[at, :] = unit_back(grad, n_ref[at, :])

    for step in range(3, chips):
        rs_slot(parts - 1, step)
    rs_finish(parts - 1)

    for part in range(parts):
        ag_drain(part)
        rs_drain(part)
        for off in range(1, chips):
            tot_copy(part, off).wait_send()
    for off in range(1, chips):
        code_copy(off).wait_send()
    for off in range(1, loops):
        pass_copy(off).wait_send()
        coef_copy(off).wait_send()
        for part in range(parts):
            query_copy(part, off).wait_send()
    pool_copy.wait_send()
    dn_copy.wait_send()


def local(queries, passages, pool, query_count, positive, neg_owner, neg_row):
    n_query, width = queries.shape
    n_pass = passages.shape[0]
    n_pool = pool.shape[0]
    hard_count = neg_owner.shape[1]
    loops = lax.axis_size("loop")
    chips = lax.axis_size("grp") // 2
    rows = n_query // parts
    lanes = chips * rows
    valid = lax.iota(jnp.int32, n_query) < query_count.reshape(())

    wanted = jnp.concatenate([neg_owner * n_pool + neg_row, positive[:, None]], axis=1)
    wanted = jnp.where(valid[:, None], wanted, -1)
    wanted = jnp.pad(wanted, ((0, 0), (0, -(hard_count + 1) % 8)), constant_values=-1)
    wanted = jnp.transpose(wanted.reshape(parts, rows, -1), (0, 2, 1))
    wanted = jnp.tile(wanted, (1, 1, chips))
    vmem = pl.BlockSpec(memory_space=pltpu.VMEM)
    dma = pltpu.SemaphoreType.DMA
    bf16, f32 = jnp.bfloat16, jnp.float32
    all_rows = 2 * n_pool + loops * n_pass
    loss, grad_query, grad_passage, grad_pool = pl.pallas_call(
        functools.partial(kernel, loops, chips, hard_count),
        out_shape=(
            jax.ShapeDtypeStruct((parts, 8, lanes), f32),
            jax.ShapeDtypeStruct((n_query, width), f32),
            jax.ShapeDtypeStruct((n_pass, width), f32),
            jax.ShapeDtypeStruct((n_pool, width), f32),
        ),
        in_specs=[vmem] * 4,
        out_specs=(vmem,) * 4,
        scratch_shapes=[
            pltpu.VMEM((parts, chips, rows, width), bf16),
            pltpu.VMEM((n_pool, width), bf16),
            pltpu.VMEM((n_pool, width), bf16),
            pltpu.VMEM((loops, n_pass, width), bf16),
            pltpu.VMEM((loops, parts, rows, width), bf16),
            pltpu.VMEM((chips,) + wanted.shape, jnp.int32),
            pltpu.VMEM((2, all_rows, lanes), f32),
            pltpu.VMEM((2 * n_pool, parts * lanes), bf16),
            pltpu.VMEM((parts, chips, 8, lanes), f32),
            pltpu.VMEM((parts, chips, rows, width), bf16),
            pltpu.VMEM((parts, chips + 1, rows, width), bf16),
            pltpu.VMEM((loops, n_pass, n_query), bf16),
            pltpu.VMEM((loops, n_pass, n_query), bf16),
            pltpu.VMEM((n_pool, width), bf16),
            pltpu.VMEM((n_pool, width), bf16),
            dma((parts, chips, 2)),
            dma((parts, chips)),
            dma((parts, chips)),
            dma((parts, chips + 1)),
            dma((parts, chips)),
            dma((parts, chips)),
            dma((chips,)),
            dma((chips,)),
            dma((loops,)),
            dma((loops,)),
            dma((parts, loops)),
            dma((parts, loops)),
            dma((loops,)),
            dma((loops,)),
            dma((2,)),
            dma((2,)),
        ],
        compiler_params=pltpu.CompilerParams(
            collective_id=0, has_side_effects=True, vmem_limit_bytes=63 * 1024 * 1024
        ),
    )(queries, passages, pool, wanted)
    loss = jnp.sum(loss[:, 0, :].reshape(parts, chips, rows), axis=1).reshape(n_query)
    return (loss, grad_query, grad_passage, grad_pool)


def solution(mesh):
    return jax.shard_map(
        local,
        mesh=mesh,
        in_specs=(
            P(("loop", "grp"), None),
            P(("loop", "grp"), None),
            P(("loop", "grp"), None),
            P("loop", "grp"),
            P(("loop", "grp")),
            P(("loop", "grp"), None),
            P(("loop", "grp"), None),
        ),
        out_specs=(
            P(("loop", "grp")),
            P(("loop", "grp"), None),
            P(("loop", "grp"), None),
            P(("loop", "grp"), None),
        ),
        check_vma=False,
    )
```

```python
import functools

import jax
import jax.numpy as jnp
from jax import lax
from jax.experimental import pallas as pl
from jax.experimental.pallas import tpu as pltpu
from jax.sharding import PartitionSpec as P

inv_temp = 50.0
eps = 1e-06
parts = 4
ahead = 2
tile = 1024
strip = 16


def scale_of(rows):
    return lax.rsqrt(jnp.sum(rows * rows, axis=-1, keepdims=True) + eps)


def unit_back(grad, raw):
    raw = raw.astype(jnp.float32)
    scale = scale_of(raw)
    unit = raw * scale
    return (grad - unit * jnp.sum(unit * grad, axis=-1, keepdims=True)) * scale


def cross(left, right):
    return lax.dot_general(
        left, right, (((1,), (1,)), ((), ())), preferred_element_type=jnp.float32
    )


def plain(left, right):
    return jnp.dot(left, right, preferred_element_type=jnp.float32)


def kernel(
    loops, chips, hard_count,
    q_ref, p_ref, n_ref, code_ref,
    loss_ref, dq_ref, dp_ref, dn_ref,
    q_all, n_own, n_sib, p_all, q_loop, codes, weights, coef, totals,
    d_part, d_recv, c_part, c_recv, dn_part, dn_recv,
    ag_s, ag_r, rs_s, rs_r, tot_s, tot_r, code_s, code_r,
    p_s, p_r, ql_s, ql_r, c_s, c_r, sib_s, sib_r,
):
    loop = lax.axis_index("loop")
    me = lax.axis_index("grp")
    z = me // 2
    core = me % 2
    sib = z * 2 + 1 - core
    n_query, width = q_ref.shape
    n_pass = p_ref.shape[0]
    n_pool = n_ref.shape[0]
    rows = n_query // parts
    lanes = chips * rows
    passages = loops * n_pass
    tiles = width // tile

    def at_chip(chip):
        return (loop, chip * 2 + core)

    def peer_chip(off):
        return lax.rem(z + off, chips)

    def peer_loop(off):
        return lax.rem(loop + off, loops)

    def remote(src, dst, send, recv, device):
        return pltpu.make_async_remote_copy(
            src_ref=src, dst_ref=dst, send_sem=send, recv_sem=recv,
            device_id=device, device_id_type=pl.DeviceIdType.MESH,
        )

    barrier = pltpu.get_barrier_semaphore()
    for off in range(1, chips):
        pl.semaphore_signal(barrier, inc=1, device_id=at_chip(peer_chip(off)),
                            device_id_type=pl.DeviceIdType.MESH)
    for off in range(1, loops):
        pl.semaphore_signal(barrier, inc=1, device_id=(peer_loop(off), me),
                            device_id_type=pl.DeviceIdType.MESH)
    pl.semaphore_signal(barrier, inc=1, device_id=(loop, sib),
                        device_id_type=pl.DeviceIdType.MESH)

    def unit_strip(raw):
        raw = raw.astype(jnp.float32)
        return (raw * scale_of(raw)).astype(jnp.bfloat16)

    def unit_queries(part):
        for low in range(0, rows, strip):
            q_all[part, z, low:low + strip, :] = unit_strip(
                q_ref[part * rows + low:part * rows + low + strip, :])

    unit_queries(0)
    pl.semaphore_wait(barrier, chips + loops - 1)

    def ag_copy(part, block, up):
        way = 0 if up else 1
        chip = z + 1 if up else z - 1
        return remote(q_all.at[part, block], q_all.at[part, block], ag_s.at[part, block, way],
                      ag_r.at[part, block], at_chip(chip))

    def ag_own(part):
        @pl.when((z < chips - 1) & (z > 0))
        def _():
            ag_copy(part, z, True).start()
            ag_copy(part, z, False).start()

    def ag_ends(part):
        @pl.when(z == 0)
        def _():
            ag_copy(part, z, True).start()

        @pl.when(z == chips - 1)
        def _():
            ag_copy(part, z, False).start()

    def ag_slot(part, step):
        @pl.when(z - step >= 0)
        def _():
            ag_copy(part, z - step, True).wait_recv()

            @pl.when(z < chips - 1)
            def _():
                ag_copy(part, z - step, True).start()

        @pl.when(z + step < chips)
        def _():
            ag_copy(part, z + step, False).wait_recv()

            @pl.when(z > 0)
            def _():
                ag_copy(part, z + step, False).start()

    def ag_drain(part):
        for step in range(chips):
            @pl.when((z - step >= 0) & (z < chips - 1))
            def _():
                ag_copy(part, z - step, True).wait_send()

            @pl.when((z + step < chips) & (z > 0))
            def _():
                ag_copy(part, z + step, False).wait_send()

    def rs_up(part, target):
        return remote(d_part.at[part, target], d_recv.at[part, target],
                      rs_s.at[part, target], rs_r.at[part, target], at_chip(z + 1))

    def rs_down(part, target):
        slot = jnp.where(target == z - 1, chips, target)
        return remote(d_part.at[part, target], d_recv.at[part, slot],
                      rs_s.at[part, target], rs_r.at[part, slot], at_chip(z - 1))

    def rs_arrived(part, slot):
        remote(d_part.at[part, 0], d_recv.at[part, slot],
               rs_s.at[part, 0], rs_r.at[part, slot], at_chip(z)).wait_recv()

    def rs_start(part):
        @pl.when(z == 0)
        def _():
            for target in range(chips - 1, 0, -1):
                rs_up(part, target).start()

        @pl.when(z == chips - 1)
        def _():
            for target in range(chips - 1):
                rs_down(part, target).start()

    def rs_add(part, target):
        d_part[part, target] = (
            d_part[part, target].astype(jnp.float32) + d_recv[part, target].astype(jnp.float32)
        ).astype(jnp.bfloat16)

    def rs_slot(part, step):
        @pl.when((z >= 1) & (step >= z))
        def _():
            target = chips - 1 - step + z
            rs_arrived(part, target)

            @pl.when(target > z)
            def _():
                rs_add(part, target)
                rs_up(part, target).start()

        @pl.when((z < chips - 1) & (step >= chips - 1 - z))
        def _():
            target = step - (chips - 1) + z
            rs_arrived(part, jnp.where(target == z, chips, target))

            @pl.when(target < z)
            def _():
                rs_add(part, target)
                rs_down(part, target).start()

    def rs_finish(part):
        dq_ref[pl.ds(part * rows, rows), :] = d_part[part, z].astype(jnp.float32)

        @pl.when(z > 0)
        def _():
            dq_ref[pl.ds(part * rows, rows), :] += d_recv[part, z].astype(jnp.float32)

        @pl.when(z < chips - 1)
        def _():
            dq_ref[pl.ds(part * rows, rows), :] += d_recv[part, chips].astype(jnp.float32)

        for low in range(part * rows, (part + 1) * rows, strip):
            at = pl.ds(low, strip)
            dq_ref[at, :] = unit_back(inv_temp * dq_ref[at, :], q_ref[at, :])

    def rs_drain(part):
        for target in range(chips):
            @pl.when(z != target)
            def _():
                rs_up(part, target).wait_send()

    def tot_copy(part, off):
        return remote(totals.at[part, z], totals.at[part, z], tot_s.at[part, off],
                      tot_r.at[part, z], at_chip(peer_chip(off)))

    def code_copy(off):
        return remote(code_ref, codes.at[z], code_s.at[off], code_r.at[z],
                      at_chip(peer_chip(off)))

    def pass_copy(off):
        return remote(p_all.at[loop], p_all.at[loop], p_s.at[off], p_r.at[loop],
                      (peer_loop(off), me))

    def query_copy(part, off):
        return remote(q_all.at[part, z], q_loop.at[loop, part], ql_s.at[part, off],
                      ql_r.at[part, loop], (peer_loop(off), me))

    def coef_copy(off):
        to = peer_loop(off)
        return remote(c_part.at[to], c_recv.at[loop], c_s.at[off], c_r.at[loop], (to, me))

    pool_copy = remote(n_own, n_sib, sib_s.at[0], sib_r.at[0], (loop, sib))
    dn_copy = remote(dn_part, dn_recv, sib_s.at[1], sib_r.at[1], (loop, sib))

    def q_cols(part, cols):
        return q_all[part, :, :, cols].reshape(lanes, tile)

    def p_cols(cols):
        return p_all[:, :, cols].reshape(passages, tile)

    def columns(i):
        return pl.ds(pl.multiple_of(i * tile, tile), tile)

    ag_own(0)
    ag_ends(0)
    for off in range(1, chips):
        code_copy(off).start()

    @pl.loop(0, n_pass // strip)
    def _(i):
        at = pl.ds(pl.multiple_of(i * strip, strip), strip)
        p_all[loop, at, :] = unit_strip(p_ref[at, :])

    for off in range(1, loops):
        pass_copy(off).start()
    unit_queries(1)
    codes[z] = code_ref[...]
    ag_ends(1)
    ag_slot(0, 1)
    ag_own(1)
    for part in range(2, parts):
        unit_queries(part)
        ag_ends(part)
    for step in range(2, chips):
        ag_slot(0, step)

    @pl.loop(0, n_pool // strip)
    def _(i):
        at = pl.ds(pl.multiple_of(i * strip, strip), strip)
        n_own[at, :] = unit_strip(n_ref[at, :])

    pool_copy.start()
    for part in range(1, ahead):
        ag_slot(part, 1)
        ag_own(part + 1)
        for step in range(2, chips):
            ag_slot(part, step)
    for part in range(parts):
        q_loop[loop, part] = q_all[part, z]
    for off in range(1, chips):
        chip = peer_chip(off)
        remote(code_ref, codes.at[chip], code_s.at[off], code_r.at[chip],
               at_chip(chip)).wait_recv()
    pool_copy.wait_recv()
    for off in range(1, loops):
        other = peer_loop(off)
        remote(p_all.at[other], p_all.at[other], p_s.at[off], p_r.at[other],
               (other, me)).wait_recv()

    own_lane = lax.broadcasted_iota(jnp.int32, (1, lanes), 1) // rows == z
    top, bottom, end = n_pool, 2 * n_pool, 2 * n_pool + passages
    c_sum = jnp.zeros((passages, n_query), jnp.float32)

    for part in range(parts):
        def add_scores(i, carry):
            cols = columns(i)
            q_tile = q_cols(part, cols)
            return (
                carry[0] + cross(n_own[:, cols], q_tile),
                carry[1] + cross(n_sib[:, cols], q_tile),
                carry[2] + cross(p_cols(cols), q_tile),
            )

        s_own, s_sib, s_in = lax.fori_loop(
            0, tiles, add_scores,
            (jnp.zeros((n_pool, lanes), jnp.float32), jnp.zeros((n_pool, lanes), jnp.float32),
             jnp.zeros((passages, lanes), jnp.float32)),
        )
        part_codes = codes[0, part]
        for chip in range(1, chips):
            here = lax.broadcasted_iota(jnp.int32, part_codes.shape, 1) // rows == chip
            part_codes = jnp.where(here, codes[chip, part], part_codes)
        row_id = lax.broadcasted_iota(jnp.int32, (n_pool, lanes), 0)
        for first, owner, score in ((0, me, s_own), (top, sib, s_sib)):
            ids = row_id + owner * n_pool
            count = jnp.zeros((n_pool, lanes), jnp.float32)
            for k in range(hard_count):
                count += jnp.where(part_codes[k:k + 1, :] == ids, 1.0, 0.0)
            weights[0, first:first + n_pool, :] = count
            weights[1, first:first + n_pool, :] = jnp.exp(score * inv_temp - inv_temp)
        s_in = s_in * inv_temp
        positive = code_ref[part, hard_count:hard_count + 1, :]
        weights[1, bottom:end, :] = jnp.exp(s_in - inv_temp)
        target = lax.broadcasted_iota(jnp.int32, (passages, lanes), 0) == positive
        chosen = jnp.sum(jnp.where(target, s_in, 0.0), axis=0, keepdims=True)
        in_total = jnp.sum(weights[1, bottom:end, :], axis=0, keepdims=True)
        hard_total = jnp.sum(weights[0, 0:bottom, :] * weights[1, 0:bottom, :], axis=0,
                             keepdims=True)
        mine = hard_total + jnp.where(own_lane, in_total, 0.0)
        totals[part, z] = jnp.broadcast_to(mine, (8, lanes))
        for off in range(1, chips):
            tot_copy(part, off).start()

        for off in range(1, loops):
            query_copy(part, off).start()
        if part >= 1:
            rs_slot(part - 1, 1)
        if part + ahead < parts:
            ag_slot(part + ahead, 1)
        if part >= 1 and chips > 2:
            rs_slot(part - 1, 2)

        for off in range(1, chips):
            chip = peer_chip(off)
            remote(totals.at[part, z], totals.at[part, chip], tot_s.at[part, off],
                   tot_r.at[part, chip], at_chip(chip)).wait_recv()
        total = totals[part, 0, 0:1, :]
        for chip in range(1, chips):
            total = total + totals[part, chip, 0:1, :]
        live = jnp.where(positive >= 0, 1.0, 0.0)
        loss_ref[part] = jnp.broadcast_to(
            jnp.where(own_lane, live * (jnp.log(total) + inv_temp - chosen), 0.0), (8, lanes)
        )
        share = weights[1, 0:bottom, :] / total
        share = share.astype(jnp.bfloat16).astype(jnp.float32) * weights[0, 0:bottom, :]
        inside = weights[1, bottom:end, :] / total - jnp.where(target, 1.0, 0.0)
        inside = jnp.where(own_lane, live * inside, 0.0)
        place = pl.ds(part * lanes, lanes)
        coef[0:bottom, place] = share.astype(jnp.bfloat16)
        pick = lax.broadcasted_iota(jnp.int32, (lanes, n_query), 0) % rows + part * rows
        pick = jnp.where(pick == lax.broadcasted_iota(jnp.int32, (lanes, n_query), 1), 1.0, 0.0)
        c_sum = c_sum + plain(inside.astype(jnp.bfloat16), pick.astype(jnp.bfloat16))
        back = jnp.transpose(share).astype(jnp.bfloat16)
        back_in = jnp.transpose(inside).astype(jnp.bfloat16)

        @pl.loop(0, tiles)
        def _(i):
            cols = columns(i)
            grad = plain(back[:, 0:top], n_own[:, cols])
            grad += plain(back[:, top:bottom], n_sib[:, cols])
            grad += plain(back_in, p_cols(cols))
            d_part[part, :, :, cols] = grad.astype(jnp.bfloat16).reshape(chips, rows, tile)

        rs_start(part)
        if part + ahead + 1 < parts:
            ag_own(part + ahead + 1)
        if part >= 1:
            for step in range(3, chips):
                rs_slot(part - 1, step)
        if part + ahead < parts:
            for step in range(2, chips):
                ag_slot(part + ahead, step)

    def q_whole(cols):
        return q_all[:, :, :, cols].reshape(parts * lanes, tile)

    c_part[...] = c_sum.astype(jnp.bfloat16).reshape(loops, n_pass, n_query)
    c_recv[loop] = c_part[loop]
    for off in range(1, loops):
        coef_copy(off).start()

    @pl.loop(0, tiles)
    def _(i):
        cols = columns(i)
        dn_part[:, cols] = plain(coef[top:bottom, :], q_whole(cols)).astype(jnp.bfloat16)

    dn_copy.start()
    rs_slot(parts - 1, 1)

    @pl.loop(0, tiles)
    def _(i):
        cols = columns(i)
        dn_ref[:, cols] = plain(coef[0:top, :], q_whole(cols))

    if chips > 2:
        rs_slot(parts - 1, 2)
    for part in range(parts - 1):
        rs_finish(part)
    for off in range(1, loops):
        other = peer_loop(off)
        remote(c_part.at[other], c_recv.at[other], c_s.at[off], c_r.at[other],
               (other, me)).wait_recv()
        for part in range(parts):
            remote(q_all.at[part, z], q_loop.at[other, part], ql_s.at[part, off],
                   ql_r.at[part, other], (other, me)).wait_recv()

    @pl.loop(0, tiles)
    def _(i):
        cols = columns(i)
        grad = jnp.zeros((n_pass, tile), jnp.float32)
        for other in range(loops):
            grad += plain(c_recv[other], q_loop[other, :, :, cols].reshape(n_query, tile))
        dp_ref[:, cols] = inv_temp * grad

    @pl.loop(0, n_pass // strip)
    def _(i):
        at = pl.ds(pl.multiple_of(i * strip, strip), strip)
        dp_ref[at, :] = unit_back(dp_ref[at, :], p_ref[at, :])

    dn_copy.wait_recv()

    @pl.loop(0, n_pool // strip)
    def _(i):
        at = pl.ds(pl.multiple_of(i * strip, strip), strip)
        grad = inv_temp * (dn_ref[at, :] + dn_recv[at, :].astype(jnp.float32))
        dn_ref[at, :] = unit_back(grad, n_ref[at, :])

    for step in range(3, chips):
        rs_slot(parts - 1, step)
    rs_finish(parts - 1)

    for part in range(parts):
        ag_drain(part)
        rs_drain(part)
        for off in range(1, chips):
            tot_copy(part, off).wait_send()
    for off in range(1, chips):
        code_copy(off).wait_send()
    for off in range(1, loops):
        pass_copy(off).wait_send()
        coef_copy(off).wait_send()
        for part in range(parts):
            query_copy(part, off).wait_send()
    pool_copy.wait_send()
    dn_copy.wait_send()


def local(queries, passages, pool, query_count, positive, neg_owner, neg_row):
    n_query, width = queries.shape
    n_pass = passages.shape[0]
    n_pool = pool.shape[0]
    hard_count = neg_owner.shape[1]
    loops = lax.axis_size("loop")
    chips = lax.axis_size("grp") // 2
    rows = n_query // parts
    lanes = chips * rows
    valid = lax.iota(jnp.int32, n_query) < query_count.reshape(())

    wanted = jnp.concatenate([neg_owner * n_pool + neg_row, positive[:, None]], axis=1)
    wanted = jnp.where(valid[:, None], wanted, -1)
    wanted = jnp.pad(wanted, ((0, 0), (0, -(hard_count + 1) % 8)), constant_values=-1)
    wanted = jnp.transpose(wanted.reshape(parts, rows, -1), (0, 2, 1))
    wanted = jnp.tile(wanted, (1, 1, chips))
    vmem = pl.BlockSpec(memory_space=pltpu.VMEM)
    dma = pltpu.SemaphoreType.DMA
    bf16, f32 = jnp.bfloat16, jnp.float32
    all_rows = 2 * n_pool + loops * n_pass
    loss, grad_query, grad_passage, grad_pool = pl.pallas_call(
        functools.partial(kernel, loops, chips, hard_count),
        out_shape=(
            jax.ShapeDtypeStruct((parts, 8, lanes), f32),
            jax.ShapeDtypeStruct((n_query, width), f32),
            jax.ShapeDtypeStruct((n_pass, width), f32),
            jax.ShapeDtypeStruct((n_pool, width), f32),
        ),
        in_specs=[vmem] * 4,
        out_specs=(vmem,) * 4,
        scratch_shapes=[
            pltpu.VMEM((parts, chips, rows, width), bf16),
            pltpu.VMEM((n_pool, width), bf16),
            pltpu.VMEM((n_pool, width), bf16),
            pltpu.VMEM((loops, n_pass, width), bf16),
            pltpu.VMEM((loops, parts, rows, width), bf16),
            pltpu.VMEM((chips,) + wanted.shape, jnp.int32),
            pltpu.VMEM((2, all_rows, lanes), f32),
            pltpu.VMEM((2 * n_pool, parts * lanes), bf16),
            pltpu.VMEM((parts, chips, 8, lanes), f32),
            pltpu.VMEM((parts, chips, rows, width), bf16),
            pltpu.VMEM((parts, chips + 1, rows, width), bf16),
            pltpu.VMEM((loops, n_pass, n_query), bf16),
            pltpu.VMEM((loops, n_pass, n_query), bf16),
            pltpu.VMEM((n_pool, width), bf16),
            pltpu.VMEM((n_pool, width), bf16),
            dma((parts, chips, 2)),
            dma((parts, chips)),
            dma((parts, chips)),
            dma((parts, chips + 1)),
            dma((parts, chips)),
            dma((parts, chips)),
            dma((chips,)),
            dma((chips,)),
            dma((loops,)),
            dma((loops,)),
            dma((parts, loops)),
            dma((parts, loops)),
            dma((loops,)),
            dma((loops,)),
            dma((2,)),
            dma((2,)),
        ],
        compiler_params=pltpu.CompilerParams(
            collective_id=0, has_side_effects=True, vmem_limit_bytes=63 * 1024 * 1024
        ),
    )(queries, passages, pool, wanted)
    loss = jnp.sum(loss[:, 0, :].reshape(parts, chips, rows), axis=1).reshape(n_query)
    return (loss, grad_query, grad_passage, grad_pool)


def solution(mesh):
    return jax.shard_map(
        local,
        mesh=mesh,
        in_specs=(
            P(("loop", "grp"), None),
            P(("loop", "grp"), None),
            P(("loop", "grp"), None),
            P("loop", "grp"),
            P(("loop", "grp")),
            P(("loop", "grp"), None),
            P(("loop", "grp"), None),
        ),
        out_specs=(
            P(("loop", "grp")),
            P(("loop", "grp"), None),
            P(("loop", "grp"), None),
            P(("loop", "grp"), None),
        ),
        check_vma=False,
    )
```
